32 devices in a mesh: group: 2 (over x), expert: 8 (over z, y), tensor: 2 (over core).
Axes of the slice: x: 2, y: 2, z: 4, core: 2. Of those that a mesh axis runs over, the one named last changes fastest.
Arguments:
- tokens: bfloat16 [2048, 3584], P(('group', 'expert', 'tensor')), parts along dimension 0, may hold values from -6 to 6
- route_ids: int32 [2048, 8], P(('group', 'expert', 'tensor')), parts along dimension 0, may hold values from 0 to 31, all different within a row; in each aligned block of 64 rows (0 to 63, 64 to 127, ...) at most 18 rows name the same one
- route_gates: float32 [2048, 8], P(('group', 'expert', 'tensor')), parts along dimension 0, may hold values from 0.1 to 0.6
- expert_gate: bfloat16 [32, 3584, 1024], P('expert', None, 'tensor'), may hold values from -0.09375 to 0.09375
- expert_up: bfloat16 [32, 3584, 1024], P('expert', None, 'tensor'), may hold values from -0.09375 to 0.09375
- expert_down: bfloat16 [32, 1024, 3584], P('expert', 'tensor'), may hold values from -0.1875 to 0.1875
- shared_gate: bfloat16 [3584, 1024], P('expert', 'tensor'), may hold values from -0.09375 to 0.09375
- shared_up: bfloat16 [3584, 1024], P('expert', 'tensor'), may hold values from -0.09375 to 0.09375
- shared_down: bfloat16 [1024, 3584], P('tensor', 'expert'), may hold values from -0.1875 to 0.1875
Outputs:
- mixed: bfloat16 [2048, 3584], P(('group', 'expert', 'tensor')), parts along dimension 0
The draws below stay inside these ranges and needn't reach their ends.
There are 2 independent parts, one for each index of `group`. The reference program is written for one: setup_inputs(seed, part) draws one part's arguments, and reference() takes and returns one part's arrays. A program takes and returns all parts, laid end to end along the dimension named above; an argument that names none is the same for every part. Nothing has to cross between parts.
Inputs may be any that keep to these rules, and one draw needn't show every extreme that they name: `route_ids`: each row names 8 different experts; among the 64 rows of one device no expert is named by more than 18 rows, and in every draw some expert is named by exactly 18 rows of some device.
All inputs are finite; a program needn't handle non-finite values.
Results may differ from the reference program's by a relative error of at most 0.006.
Values may be sent and summed in bfloat16 or wider, within the bound.
No kernel may reach another device: no remote copies, remote signals or barrier semaphores. Data moves between devices by JAX's collectives and lax.ppermute only.
A program may use at most 192 MiB of HBM per device.

```python
import math
import jax
import jax.numpy as jnp
import numpy as np
from jax import lax

D = 3584
RH = 1024
SH = 1024
EXPERTS = 32
TOP = 8
TOK_DEV = 64
MOST = 18
TOKENS = 1024
N_EXPERT = 8
N_TENSOR = 2


def level_of(own_key, extent, pieces, smallest, largest):
    def one(axis_at, blocks):
        steps = jax.random.uniform(jax.random.fold_in(jax.random.fold_in(own_key, 6), axis_at), (blocks,), jnp.float32, smallest / len(pieces), largest / len(pieces))
        return jnp.repeat(jnp.exp(steps), extent[axis_at] // blocks).reshape((-1,) + (1,) * (len(extent) - axis_at - 1))

    level = one(*pieces[0])
    for cut in pieces[1:]:
        level = level * one(*cut)
    return level


def deal_out(stream_key, own, number, rows, number_of, top, reach, skew):
    order = jax.random.permutation(stream_key, number_of)
    heavy_load, common = portions_of(number_of, rows * top, reach, skew, True), portions_of(number_of, rows * top, reach, skew, False)
    places = jnp.arange(number_of)

    def named(tallies, rotation):
        used = int((tallies > 0).sum())
        fixed = max(1, used // 4)
        shifted = fixed + (places - fixed + rotation * (used - fixed)) % max(1, number_of - fixed)
        return jnp.zeros((number_of,), jnp.int32).at[order[jnp.where(places < fixed, places, shifted)]].set(jnp.asarray(tallies, jnp.int32))

    tallies = jnp.where(number % 4 == 0, named(heavy_load, number // 4), named(common, number - number // 4 - 1))
    mixed = jax.random.permutation(jax.random.fold_in(own, 3), number_of)
    giver, sink = mixed[0:number_of // 2 * 2:2], mixed[1:number_of // 2 * 2:2]
    room = jnp.minimum(tallies[giver] - 1, reach - tallies[sink]) // 2
    room = jnp.where((giver == order[0]) | (sink == order[0]) | (tallies[sink] == 0), 0, jnp.maximum(room, 0))
    shifted = jax.random.randint(jax.random.fold_in(own, 4), (number_of // 2,), 0, 1 << 20) % (room + 1)
    tallies = tallies.at[giver].add(-shifted).at[sink].add(shifted)
    labels = jnp.searchsorted(jnp.cumsum(tallies), jnp.arange(rows * top), side="right").astype(jnp.int32)
    listing = labels.reshape(top, rows).T
    listing = listing[jax.random.permutation(jax.random.fold_in(own, 1), rows)]
    rotation = jax.random.randint(jax.random.fold_in(own, 2), (rows, 1), 0, top)
    return jnp.take_along_axis(listing, (jnp.arange(top)[None, :] + rotation) % top, axis=1)


def portions_of(count, total, reach, slope, full):
    loads = [(1 << 20) // math.isqrt(grade ** slope) + 1 for grade in range(1, count + 1)]
    largest = reach if full else min(reach, max(-(-total // count), total * loads[0] // sum(loads)))
    least = 1 if total - largest >= count - 1 else 0
    given, rest = [largest] + [least] * (count - 1), total - largest - least * (count - 1)
    while rest > 0:
        movable = [i for i in range(1, count) if given[i] < largest] or [i for i in range(1, count) if given[i] < reach]
        pool, remaining = sum([loads[i] for i in movable]), rest
        for i in movable:
            more = min(reach - given[i], max(1, remaining * loads[i] // pool), rest)
            given[i] = given[i] + more
            rest = rest - more
    return np.array(given)


def scatter_about(stream_key, dims, spread, most, shards=(), kind=jnp.bfloat16):
    values = spread * jax.random.normal(stream_key, dims, jnp.float32)
    if shards:
        values = values * level_of(stream_key, dims, shards, -0.22, 0.18)
    return jnp.clip(values, -most, most).astype(kind)


def setup_inputs(seed: int = 0, part: int = 0) -> dict:
    keys = jax.random.split(jax.random.key(seed), 10)
    own_keys = jax.random.split(jax.random.fold_in(keys[9], part), 10)
    tokens = scatter_about(own_keys[0], (TOKENS, D), 1.0, 6.0, ((0, 16),))
    route_ids_keys = jax.random.split(jax.random.fold_in(own_keys[1], 1), TOKENS // TOK_DEV)
    route_ids_turns = jax.random.permutation(jax.random.fold_in(own_keys[1], 3), TOKENS // TOK_DEV)
    route_ids = jax.vmap(lambda own, number: deal_out(jax.random.fold_in(own_keys[1], 2), own, number, TOK_DEV, EXPERTS, TOP, MOST, 2))(route_ids_keys, route_ids_turns).reshape((TOKENS, TOP))
    route_gates = jnp.clip(0.1 + 0.5 * jax.random.uniform(own_keys[2], (TOKENS, TOP), jnp.float32) ** level_of(own_keys[2], (TOKENS, TOP), ((0, 16),), -0.2, 0.2), 0.1, 0.6)
    expert_gate = scatter_about(keys[3], (EXPERTS, D, RH), D ** -0.5, 0.09375, ((0, 8), (2, 2)))
    expert_up = scatter_about(keys[4], (EXPERTS, D, RH), D ** -0.5, 0.09375, ((0, 8), (2, 2)))
    expert_down = scatter_about(keys[5], (EXPERTS, RH, D), RH ** -0.5, 0.1875, ((0, 8), (1, 2)))
    shared_gate = scatter_about(keys[6], (D, SH), D ** -0.5, 0.09375, ((0, 8), (1, 2)))
    shared_up = scatter_about(keys[7], (D, SH), D ** -0.5, 0.09375, ((0, 8), (1, 2)))
    shared_down = scatter_about(keys[8], (SH, D), SH ** -0.5, 0.1875, ((0, 2), (1, 8)))
    return dict(tokens=tokens, route_ids=route_ids, route_gates=route_gates, expert_gate=expert_gate, expert_up=expert_up, expert_down=expert_down, shared_gate=shared_gate, shared_up=shared_up, shared_down=shared_down)


def reference(tokens, route_ids, route_gates, expert_gate, expert_up, expert_down, shared_gate, shared_up, shared_down):
    total = tokens.shape[0]
    shared_gated = jnp.dot(tokens, shared_gate, preferred_element_type=jnp.float32)
    shared_upward = jnp.dot(tokens, shared_up, preferred_element_type=jnp.float32)
    shared_hidden = (jax.nn.silu(shared_gated) * shared_upward).astype(jnp.bfloat16)
    shared_out = jnp.dot(shared_hidden, shared_down, preferred_element_type=jnp.float32)

    flat_ids = route_ids.reshape(-1).astype(jnp.int32)
    route_total = flat_ids.shape[0]
    order = jnp.argsort(flat_ids, stable=True).astype(jnp.int32)
    counts = jnp.sum((flat_ids[None, :] == jnp.arange(EXPERTS, dtype=jnp.int32)[:, None]).astype(jnp.int32), axis=1).astype(jnp.int32)
    starts = (jnp.cumsum(counts) - counts).astype(jnp.int32)
    limit = N_EXPERT * N_TENSOR * MOST
    padded = jnp.concatenate([order, jnp.zeros((limit,), jnp.int32)])
    piece = RH // N_TENSOR

    def one_expert(expert):
        picks = lax.dynamic_slice(padded, (starts[expert].astype(jnp.int32),), (limit,))
        live = jnp.arange(limit, dtype=jnp.int32) < counts[expert]
        rows = tokens[picks // TOP]
        gated = jnp.dot(rows, expert_gate[expert], preferred_element_type=jnp.float32)
        upward = jnp.dot(rows, expert_up[expert], preferred_element_type=jnp.float32)
        hidden = (jax.nn.silu(gated) * upward).astype(jnp.bfloat16)
        down = expert_down[expert]
        summed = jnp.zeros((limit, D), jnp.float32)
        for half in range(N_TENSOR):
            part = jnp.dot(hidden[:, half * piece:(half + 1) * piece], down[half * piece:(half + 1) * piece], preferred_element_type=jnp.float32)
            summed = summed + lax.optimization_barrier(part.astype(jnp.bfloat16)).astype(jnp.float32)
        outcome = lax.optimization_barrier(summed.astype(jnp.bfloat16)).astype(jnp.float32)
        outcome = jnp.where(live[:, None], outcome, jnp.zeros_like(outcome))
        return outcome, picks

    outcomes, picks = lax.map(one_expert, jnp.arange(EXPERTS, dtype=jnp.int32))
    route_out = jnp.zeros((route_total, D), jnp.float32).at[picks.reshape(-1)].add(outcomes.reshape(-1, D))
    weighted = route_out.reshape(total, TOP, D) * route_gates.astype(jnp.float32)[:, :, None]
    routed = jnp.sum(weighted, axis=1)
    return (routed + shared_out).astype(jnp.bfloat16)
```

```python
import functools

import jax
import jax.numpy as jnp
import numpy as np
from jax import lax
from jax.experimental import pallas as pl
from jax.experimental.pallas import tpu as pltpu
from jax.sharding import PartitionSpec as P

MOST = 18
LANES = 128
MIB = 1 << 20
BF16 = jnp.bfloat16
F32 = jnp.float32


def cost(flops, moved):
    return pl.CostEstimate(flops=int(flops), bytes_accessed=int(moved), transcendentals=0)


def params(mib):
    return pltpu.CompilerParams(vmem_limit_bytes=mib * MIB)


def column_tiles(total, width=512):
    return [(at, min(width, total - at)) for at in range(0, total, width)]


def silu(value):
    return value * (1.0 / (1.0 + jnp.exp(-value)))


def pick_kernel(count, *refs):
    picks, tokens, out = refs[0], refs[1 : 1 + count], refs[1 + count]
    experts, slots, features = out.shape
    which = picks[0]
    for at, width in column_tiles(features):
        piece = jnp.concatenate([t[:, at : at + width] for t in tokens], axis=0)
        rows = jnp.dot(which, piece, preferred_element_type=F32).astype(BF16)
        out[:, :, at : at + width] = rows.reshape(experts, slots, width)


def pick_rows(picks, chunk, tokens, experts):
    slots, width = picks.shape[1:]
    features = tokens[0].shape[1]
    return pl.pallas_call(
        functools.partial(pick_kernel, len(tokens)),
        out_shape=jax.ShapeDtypeStruct((experts, slots // experts, features), BF16),
        grid=(1,),
        in_specs=[pl.BlockSpec((1, slots, width), lambda i: (chunk, 0, 0))]
        + [pl.BlockSpec(t.shape, lambda i: (0, 0)) for t in tokens],
        out_specs=pl.BlockSpec((experts, slots // experts, features), lambda i: (0, 0, 0)),
        compiler_params=params(24),
        cost_estimate=cost(2 * slots * width * features, 2 * features * (slots + width)),
        name="pick_rows",
    )(picks, *tokens)


def expert_kernel(count, *refs):
    rows_in, (scale, gate, up, down) = refs[:count], refs[count : count + 4]
    rows_out, (rows, total) = refs[count + 4 : 2 * count + 4], refs[2 * count + 4 :]
    slots = rows_in[0].shape[1]
    features = rows.shape[1]
    step = pl.program_id(1)

    @pl.when(step == 0)
    def _():
        for i, r in enumerate(rows_in):
            rows[i * slots : (i + 1) * slots, :] = r[0]

    value = rows[...]
    gated = jnp.dot(value, gate[0], preferred_element_type=F32)
    upward = jnp.dot(value, up[0], preferred_element_type=F32)
    hidden = (silu(gated) * upward * scale[0]).astype(BF16)

    @pl.when(step == 0)
    def _():
        for at, width in column_tiles(features):
            total[:, at : at + width] = jnp.dot(
                hidden, down[0, :, at : at + width], preferred_element_type=F32
            )

    @pl.when(step == 1)
    def _():
        for at, width in column_tiles(features):
            done = total[:, at : at + width] + jnp.dot(
                hidden, down[0, :, at : at + width], preferred_element_type=F32
            )
            done = done.astype(BF16)
            for i, r in enumerate(rows_out):
                r[0, :, at : at + width] = done[i * slots : (i + 1) * slots]


def run_experts(rows, scale, gate, up, down):
    experts, slots, features = rows[0].shape
    hidden = gate.shape[2]
    tile = hidden // 2
    count = len(rows)
    height = count * slots
    spec = pl.BlockSpec((1, slots, features), lambda e, h: (e, 0, 0))
    return pl.pallas_call(
        functools.partial(expert_kernel, count),
        out_shape=[jax.ShapeDtypeStruct(r.shape, BF16) for r in rows],
        grid=(experts, 2),
        in_specs=[spec] * count
        + [
            pl.BlockSpec((1, height, 1), lambda e, h: (e, 0, 0)),
            pl.BlockSpec((1, features, tile), lambda e, h: (e, 0, h)),
            pl.BlockSpec((1, features, tile), lambda e, h: (e, 0, h)),
            pl.BlockSpec((1, tile, features), lambda e, h: (e, h, 0)),
        ],
        out_specs=[spec] * count,
        scratch_shapes=[pltpu.VMEM((height, features), BF16), pltpu.VMEM((height, features), F32)],
        compiler_params=params(48),
        cost_estimate=cost(
            6 * experts * height * features * hidden,
            2 * experts * features * (3 * hidden + 2 * height),
        ),
        name="run_experts",
    )(*rows, scale, gate, up, down)


def shared_kernel(count, sums, last, *refs):
    start, tokens, weight = refs[0], refs[1 : 1 + count], refs[1 + count]
    before, out = refs[2 + count : 2 + count + sums], refs[2 + count + sums]
    window = pl.ds(pl.multiple_of(start[0], LANES), weight.shape[0])
    piece = jnp.concatenate([t[:, window] for t in tokens], axis=0)
    value = jnp.dot(piece, weight[...], preferred_element_type=F32)
    for b in before:
        value = value + b[...].astype(F32)
    if last:
        half = value.shape[1] // 2
        value = silu(value[:, :half]) * value[:, half:]
    out[...] = value.astype(BF16)


def shared_term(start, tokens, weight, before, last=False):
    height = sum(t.shape[0] for t in tokens)
    width = weight.shape[1] // 2 if last else weight.shape[1]
    vmem = pl.BlockSpec(memory_space=pltpu.VMEM)
    return pl.pallas_call(
        functools.partial(shared_kernel, len(tokens), len(before), last),
        out_shape=jax.ShapeDtypeStruct((height, width), BF16),
        in_specs=[pl.BlockSpec(memory_space=pltpu.SMEM)]
        + [vmem] * (len(tokens) + 1 + len(before)),
        out_specs=vmem,
        compiler_params=params(16),
        cost_estimate=cost(
            2 * height * weight.size, 2 * (weight.size + height * (tokens[0].shape[1] + 3 * width))
        ),
        name="shared_term",
    )(start, *tokens, weight, *before)


def merge_kernel(start, picks, rows, hidden, down, own, other):
    height = own.shape[0]
    which = picks[0]
    for at, width in column_tiles(own.shape[1]):
        value = jnp.concatenate(
            [rows[e, :, at : at + width] for e in range(rows.shape[0])], axis=0
        )
        value = jnp.dot(which, value, preferred_element_type=F32)
        own[:, at : at + width] = value[:height].astype(own.dtype)
        other[:, at : at + width] = value[height:].astype(other.dtype)
    window = pl.ds(pl.multiple_of(start[0], LANES), down.shape[1])
    value = jnp.dot(hidden[...], down[...], preferred_element_type=F32)
    own[:, window] = (own[:, window].astype(F32) + value[:height]).astype(own.dtype)
    other[:, window] = (other[:, window].astype(F32) + value[height:]).astype(other.dtype)


def merge_block(start, picks, place, rows, hidden, down):
    height, slots = picks.shape[1:]
    features = rows.shape[2]
    whole = lambda a: pl.BlockSpec(a.shape, lambda i: (0,) * a.ndim)
    return pl.pallas_call(
        merge_kernel,
        out_shape=[jax.ShapeDtypeStruct((height // 2, features), BF16)] * 2,
        grid=(1,),
        in_specs=[
            pl.BlockSpec(memory_space=pltpu.SMEM),
            pl.BlockSpec((1, height, slots), lambda i: (place, 0, 0)),
            whole(rows),
            whole(hidden),
            whole(down),
        ],
        out_specs=[pl.BlockSpec((height // 2, features), lambda i: (0, 0))] * 2,
        compiler_params=params(24),
        cost_estimate=cost(2 * height * slots * features, 2 * features * (slots + 2 * height)),
        name="merge_block",
    )(start, picks, rows, hidden, down)


def window_of(count, size, total):
    need = max((i * size) % LANES + size for i in range(count))
    width = min(total, -(-need // LANES) * LANES)
    starts = np.array([min(i * size // LANES * LANES, total - width) for i in range(count)])
    return width, starts.astype(np.int32), (np.arange(count) * size - starts).astype(np.int32)


def on_device(
    tokens,
    route_ids,
    route_gates,
    expert_gate,
    expert_up,
    expert_down,
    shared_gate,
    shared_up,
    shared_down,
):
    n = lax.axis_size("expert")
    half = n // 2
    me, core = lax.axis_index("expert"), lax.axis_index("tensor")
    row_count, features = tokens.shape
    top = route_ids.shape[1]
    experts = expert_gate.shape[0]
    block = 2 * row_count

    path = np.array(list(range(0, n, 2)) + list(range(n - 1, 0, -2)), np.int32)
    onward = [(int(path[i]), int(path[(i + 1) % n])) for i in range(n)]
    backward = [(b, a) for a, b in onward]
    place = jnp.asarray(np.argsort(path).astype(np.int32))[me]
    send_on = lambda a: lax.ppermute(a, "expert", onward)
    send_back = lambda a: lax.ppermute(a, "expert", backward)
    swap = lambda a: lax.ppermute(a, "tensor", [(0, 1), (1, 0)])

    routing = jnp.concatenate([route_ids.astype(F32), route_gates], axis=1)
    routing = lax.all_gather(routing, ("expert", "tensor"), axis=0, tiled=True)
    routing = routing.reshape(n, 2, row_count, 2 * top)
    pairs = [0, half] + [p for k in range(1, half) for p in (k, n - k)]
    chunk_of = {p: i // 2 for i, p in enumerate(pairs)}
    order = jnp.asarray(path)[(place + jnp.asarray(np.array(pairs, np.int32))) % n]
    routing = routing[order]
    routing = jnp.where(core == 0, routing, routing[:, ::-1])
    routing = routing.reshape(half, 2 * block, 2 * top)
    ids, gates = routing[..., :top].astype(jnp.int32), routing[..., top:]
    local = me * experts + jnp.arange(experts, dtype=jnp.int32)
    hit = ids[:, None] == local[None, :, None, None]
    named = jnp.any(hit, axis=3)
    gate_of = jnp.sum(jnp.where(hit, gates[:, None], 0.0), axis=3)
    slots = -(-4 * MOST // 16) * 16
    upto = jnp.asarray(np.triu(np.ones((2 * block, 2 * block), np.float32)), BF16)
    rank = jnp.dot(named.astype(BF16), upto, preferred_element_type=F32).astype(jnp.int32) - 1
    first = (jnp.arange(experts, dtype=jnp.int32) * slots)[None, :, None]
    slot = jnp.where(named, rank + first, -1)
    number = jnp.arange(experts * slots, dtype=jnp.int32)
    match = slot[:, :, None, :] == number[None, None, :, None]
    picks = jnp.any(match, axis=1).astype(BF16)
    scale = jnp.sum(jnp.where(match, gate_of[:, :, None, :], 0.0), axis=(1, 3))
    scale = scale.reshape(half, experts, slots).transpose(1, 0, 2)
    scale = scale.reshape(experts, half * slots, 1)
    spread = jnp.swapaxes(slot, 1, 2)
    spread = jnp.any(spread[:, :, :, None] == number[None, None, None, :], axis=2).astype(BF16)
    spread = spread.reshape(n, block, experts * slots)

    width, starts, shifts = window_of(n, shared_gate.shape[0], features)
    start = jnp.asarray(starts)[me].reshape(1)
    shift = jnp.asarray(shifts)[me]
    zero = jnp.int32(0)
    both = jnp.concatenate([shared_gate, shared_up], axis=1)
    both = lax.dynamic_update_slice(jnp.zeros((width, both.shape[1]), BF16), both, (shift, zero))
    down = lax.dynamic_update_slice(
        jnp.zeros((shared_down.shape[0], width), BF16), shared_down, (zero, shift)
    )

    seen = {0: [tokens, swap(tokens)]}
    term = lambda r, *before, **k: shared_term(start, seen[r], both, before, **k)
    sum_on, sum_back = term(0), None
    ahead, behind = tokens, tokens
    rows = {}
    for k in range(1, half):
        ahead, behind = send_on(ahead), send_back(behind)
        seen[n - k] = [ahead, swap(ahead)]
        seen[k] = [behind, swap(behind)]
        sum_on = term(n - k, send_on(sum_on))
        sum_back = term(k) if k == 1 else term(k, send_back(sum_back))
        rows[k] = pick_rows(picks, k, seen[k] + seen[n - k], experts)
    split = row_count // 2
    ahead, behind = send_on(ahead[:split]), send_back(behind[split:])
    seen[half] = [ahead, behind, swap(ahead), swap(behind)]
    rows[0] = pick_rows(picks, 0, seen[0] + seen[half], experts)
    hidden = {half: term(half, send_on(sum_on), send_back(sum_back), last=True)}

    routed = {}
    for at in range(0, half, 4):
        group = list(range(at, min(at + 4, half)))
        part = scale[:, at * slots : (at + len(group)) * slots]
        outs = run_experts([rows[j] for j in group], part, expert_gate, expert_up, expert_down)
        routed.update(zip(group, outs))

    for k in range(1, half):
        hidden[half - k] = send_on(hidden[half - k + 1])
        hidden[half + k] = send_back(hidden[half + k - 1])
    hidden[0] = jnp.concatenate(
        [send_on(hidden[1][:row_count]), send_back(hidden[n - 1][row_count:])], axis=0
    )

    def contribution(r):
        own, other = merge_block(
            start, spread, pairs.index(r), routed[chunk_of[r]], hidden[r], down
        )
        return own.astype(F32), swap(other).astype(F32)

    own, other = contribution(half)
    ahead = send_on((own + other)[:split].astype(BF16))
    behind = send_back((own + other)[split:].astype(BF16))
    for k in range(half - 1, 0, -1):
        own, other = contribution(k)
        sent = ahead.astype(F32)
        if k == half - 1:
            sent = jnp.concatenate([sent, jnp.zeros((row_count - split, features), F32)], axis=0)
        ahead = send_on((own + other + sent).astype(BF16))
        own, other = contribution(n - k)
        sent = behind.astype(F32)
        if k == half - 1:
            sent = jnp.concatenate([jnp.zeros((split, features), F32), sent], axis=0)
        behind = send_back((own + other + sent).astype(BF16))
    own, other = contribution(0)
    return (own + other + ahead.astype(F32) + behind.astype(F32)).astype(BF16)


def solution(mesh):
    in_specs = (
        P(("group", "expert", "tensor"), None),
        P(("group", "expert", "tensor"), None),
        P(("group", "expert", "tensor"), None),
        P("expert", None, "tensor"),
        P("expert", None, "tensor"),
        P("expert", "tensor", None),
        P("expert", "tensor"),
        P("expert", "tensor"),
        P("tensor", "expert"),
    )
    out_specs = P(("group", "expert", "tensor"), None)
    return jax.shard_map(
        on_device, mesh=mesh, in_specs=in_specs, out_specs=out_specs, check_vma=False
    )
```

```python
import functools

import jax
import jax.numpy as jnp
from jax import lax
from jax.experimental import pallas as pl
from jax.experimental.pallas import tpu as pltpu
from jax.sharding import PartitionSpec as P

MOST = 18
LANES = 128
MIB = 1 << 20
BF16 = jnp.bfloat16
F32 = jnp.float32


def cost(moved=3 * 10**6):
    return pl.CostEstimate(flops=1000, bytes_accessed=moved, transcendentals=0)


def params(mib):
    return pltpu.CompilerParams(vmem_limit_bytes=mib * MIB)


def column_tiles(total, width=512):
    return [(at, min(width, total - at)) for at in range(0, total, width)]


def silu(value):
    return value * (1.0 / (1.0 + jnp.exp(-value)))


def whole(array):
    return pl.BlockSpec(array.shape, lambda i: (0,) * array.ndim)


def pick_kernel(count, experts, top, cut, first, *refs):
    tokens, out, spread = refs[:count], refs[count], refs[count + 1]
    if cut:
        tokens = [
            r if i % 2 and count == 4 else r.at[:cut] if cut > 0 else r.at[-cut:]
            for i, r in enumerate(tokens)
        ]
    features = out.shape[2]
    height, slots = spread.shape
    notes = jnp.concatenate([t[:, features - LANES :] for t in tokens], axis=0).astype(F32)
    lane = lax.broadcasted_iota(jnp.int32, notes.shape, 1)
    named = jnp.zeros(notes.shape, F32)
    for e in range(experts):
        same = (notes == (first[0] + e).astype(F32)) & (lane < top)
        hit = jnp.max(jnp.where(same, 1.0, 0.0), axis=1, keepdims=True)
        named = jnp.where(lane == e, hit, named)
    down = lax.broadcasted_iota(jnp.int32, (height, height), 0)
    across = lax.broadcasted_iota(jnp.int32, (height, height), 1)
    upto = jnp.where(across <= down, 1.0, 0.0).astype(BF16)
    rank = jnp.dot(upto, named.astype(BF16), preferred_element_type=F32).astype(jnp.int32) - 1
    slot = jnp.where(named > 0.0, rank + lane * (slots // experts), -1)
    turned = jnp.transpose(slot.astype(F32)).astype(jnp.int32)
    number = lax.broadcasted_iota(jnp.int32, (slots, height), 0)
    column = lax.broadcasted_iota(jnp.int32, (height, slots), 1)
    picks = number == turned[0:1, :]
    back = column == slot[:, 0:1]
    for e in range(1, experts):
        picks = picks | (number == turned[e : e + 1, :])
        back = back | (column == slot[:, e : e + 1])
    picks = jnp.where(picks, 1.0, 0.0).astype(BF16)
    spread[...] = jnp.where(back, 1.0, 0.0).astype(BF16)
    for at, width in column_tiles(features):
        piece = jnp.concatenate([t[:, at : at + width] for t in tokens], axis=0)
        rows = jnp.dot(picks, piece, preferred_element_type=F32).astype(BF16)
        out[:, :, at : at + width] = rows.reshape(experts, slots // experts, width)


def pick_rows(first, tokens, experts, slots, top, cut):
    height = sum(t.shape[0] for t in tokens)
    if cut > 0:
        height += sum(cut - t.shape[0] for t in tokens[::2])
    if cut < 0:
        height += cut * len(tokens)
    features = tokens[0].shape[1]
    vmem = pl.BlockSpec(memory_space=pltpu.VMEM)
    return pl.pallas_call(
        functools.partial(pick_kernel, len(tokens), experts, top, cut),
        out_shape=[
            jax.ShapeDtypeStruct((experts, slots, features), BF16),
            jax.ShapeDtypeStruct((height, experts * slots), BF16),
        ],
        in_specs=[pl.BlockSpec(memory_space=pltpu.SMEM)] + [vmem] * len(tokens),
        out_specs=[vmem, vmem],
        compiler_params=params(16),
        cost_estimate=cost(),
        name="pick_rows",
    )(first, *tokens)


def expert_kernel(count, top, first, *refs):
    rows_in, (gate, up, down) = refs[:count], refs[count : count + 3]
    rows_out, rows = refs[count + 3 : 2 * count + 3], refs[2 * count + 3]
    slots, wide = rows_in[0].shape[1:]
    features = down.shape[2]
    for i, r in enumerate(rows_in):
        rows[i * slots : (i + 1) * slots, :] = r[0]
    notes = rows[:, features:].astype(F32)
    lane = lax.broadcasted_iota(jnp.int32, notes.shape, 1)
    expert = (first[0] + pl.program_id(0)).astype(F32)
    chosen = jnp.where((notes == expert) & (lane < top), 1.0, 0.0)
    scale = jnp.zeros((notes.shape[0], 1), F32)
    for part in (1, 2, 3):
        moved = jnp.concatenate([notes[:, part * top :], notes[:, : part * top]], axis=1)
        scale = scale + jnp.sum(chosen * moved, axis=1, keepdims=True)
    value = rows[:, :features]
    gated = jnp.dot(value, gate[0], preferred_element_type=F32)
    upward = jnp.dot(value, up[0], preferred_element_type=F32)
    hidden = (silu(gated) * upward * scale).astype(BF16)
    for at, width in column_tiles(features):
        done = jnp.dot(hidden, down[0, :, at : at + width], preferred_element_type=F32)
        done = done.astype(BF16)
        for i, r in enumerate(rows_out):
            r[0, :, at : at + width] = done[i * slots : (i + 1) * slots]


def run_experts(first, rows, gate, up, down, top):
    experts, slots, wide = rows[0].shape
    features, hidden = gate.shape[1:]
    count = len(rows)
    height = count * slots
    return pl.pallas_call(
        functools.partial(expert_kernel, count, top),
        out_shape=[jax.ShapeDtypeStruct((experts, slots, features), BF16)] * count,
        grid=(experts,),
        in_specs=[pl.BlockSpec(memory_space=pltpu.SMEM)]
        + [pl.BlockSpec((1, slots, wide), lambda e: (e, 0, 0))] * count
        + [
            pl.BlockSpec((1, features, hidden), lambda e: (e, 0, 0)),
            pl.BlockSpec((1, features, hidden), lambda e: (e, 0, 0)),
            pl.BlockSpec((1, hidden, features), lambda e: (e, 0, 0)),
        ],
        out_specs=[pl.BlockSpec((1, slots, features), lambda e: (e, 0, 0))] * count,
        scratch_shapes=[pltpu.VMEM((height, wide), BF16)],
        compiler_params=params(38),
        cost_estimate=cost(7 * 10**7),
        name="run_experts",
    )(first, *rows, gate, up, down)


def first_kernel(shifts, start, shift, tokens, ids, gates, *refs):
    parts, (weight, down), sends = refs[:6], refs[6:8], refs[8:]
    height, width = parts[0].shape
    depth = parts[4].shape[1]
    gap = weight.shape[0] - height
    for s in shifts:

        @pl.when(shift[0] == s)
        def _():
            for i in range(4):
                here = slice(i * width, (i + 1) * width)
                if s:
                    weight[:s, here] = jnp.zeros((s, width), BF16)
                weight[s : s + height, here] = parts[i][...]
                if s < gap:
                    weight[s + height :, here] = jnp.zeros((gap - s, width), BF16)
            for i in range(2):
                here = slice(i * depth, (i + 1) * depth)
                if s:
                    down[:s, here] = jnp.zeros((s, depth), BF16)
                down[s : s + height, here] = parts[4 + i][...]
                if s < gap:
                    down[s + height :, here] = jnp.zeros((gap - s, depth), BF16)

    rows, features = tokens.shape
    gate = gates[...]
    high = gate.astype(BF16).astype(F32)
    middle = (gate - high).astype(BF16).astype(F32)
    low = gate - high - middle
    notes = [ids[...].astype(F32), high, middle, low]
    notes.append(jnp.zeros((LANES - 4 * ids.shape[0], rows), F32))
    notes = jnp.transpose(jnp.concatenate(notes, axis=0)).astype(BF16)
    window = pl.ds(pl.multiple_of(start[0], LANES), weight.shape[0])
    value = jnp.dot(tokens[:, window], weight[...], preferred_element_type=F32).astype(BF16)
    split = rows // 2
    wide = features + LANES
    for i, out in enumerate(sends):
        here = slice(i % 2 * split, (i % 2 + 1) * split) if i < 4 else slice(0, rows)
        out[:, :features] = tokens[here, :]
        out[:, features:wide] = notes[here]
        if i < 2:
            out[:, wide:] = value[here]


def first_step(start, shift, shifts, tokens, ids, gates, weights, width):
    rows, features = tokens.shape
    split, wide = rows // 2, features + LANES
    inner = weights[0].shape[1]
    outs = [(width, 4 * inner), (width, 2 * inner)]
    outs += [(split, wide + 4 * inner)] * 2 + [(split, wide)] * 2 + [(rows, wide)]
    outs = [jax.ShapeDtypeStruct(shape, BF16) for shape in outs]
    smem = pl.BlockSpec(memory_space=pltpu.SMEM)
    arrays = [tokens, ids, gates, *weights]
    return pl.pallas_call(
        functools.partial(first_kernel, shifts),
        out_shape=outs,
        grid=(1,),
        in_specs=[smem, smem] + [whole(a) for a in arrays],
        out_specs=[whole(o) for o in outs],
        compiler_params=params(60),
        cost_estimate=cost(),
        name="first_step",
    )(start, shift, *arrays)


def step_kernel(wide, sends, start, weight, on, back, *refs):
    others, outs = (refs[:-3], refs[-3:]) if len(refs) > 2 else ((), refs)
    height = on.shape[0]
    window = pl.ds(pl.multiple_of(start[0], LANES), weight.shape[0])
    piece = jnp.concatenate([on[:, window], back[:, window]], axis=0)
    value = jnp.dot(piece, weight[...], preferred_element_type=F32)
    for i, arrived in enumerate((on, back)):
        part = value[i * height : (i + 1) * height]
        if arrived.shape[1] > wide:
            part = part + arrived[:, wide:].astype(F32)
        if sends[i]:
            outs[i][:, :wide] = arrived[:, :wide]
            outs[i][:, wide:] = part.astype(BF16)
        else:
            outs[i][...] = part.astype(BF16)
    if others:
        at = 0
        for r in (*others, on, back):
            outs[2][at : at + r.shape[0], :] = r[:, :wide]
            at += r.shape[0]


def step_on(start, weight, on, back, wide, sends, others=()):
    height, width = on.shape[0], weight.shape[1]
    vmem = pl.BlockSpec(memory_space=pltpu.VMEM)
    shapes = [(height, wide + width) if full else (height, width) for full in sends]
    if others:
        shapes.append((sum(o.shape[0] for o in others) + 2 * height, wide))
    return pl.pallas_call(
        functools.partial(step_kernel, wide, sends),
        out_shape=[jax.ShapeDtypeStruct(shape, BF16) for shape in shapes],
        in_specs=[pl.BlockSpec(memory_space=pltpu.SMEM)] + [vmem] * (3 + len(others)),
        out_specs=[vmem] * len(shapes),
        compiler_params=params(16),
        cost_estimate=cost(),
        name="step_on",
    )(start, weight, on, back, *others)


def last_kernel(wide, start, weight, main, side, *refs):
    others, (units, *tokens) = (refs[:1], refs[1:]) if len(refs) == 3 else ((), refs)
    height = main.shape[0]
    window = pl.ds(pl.multiple_of(start[0], LANES), weight.shape[0])
    value = jnp.dot(main[:, window], weight[...], preferred_element_type=F32)
    value = value + main[:, wide:].astype(F32) + side[...].astype(F32)
    half = value.shape[1] // 2
    units[...] = (silu(value[:, :half]) * value[:, half:]).astype(BF16)
    if others:
        for i, r in enumerate((*others, main)):
            tokens[0][i * height : (i + 1) * height, :] = r[:, :wide]


def last_step(start, weight, main, side, wide, others=()):
    height = main.shape[0]
    vmem = pl.BlockSpec(memory_space=pltpu.VMEM)
    return pl.pallas_call(
        functools.partial(last_kernel, wide),
        out_shape=[jax.ShapeDtypeStruct((height, weight.shape[1] // 2), BF16)]
        + [jax.ShapeDtypeStruct((2 * height, wide), BF16)] * len(others),
        in_specs=[pl.BlockSpec(memory_space=pltpu.SMEM)] + [vmem] * (3 + len(others)),
        out_specs=[vmem] * (1 + len(others)),
        compiler_params=params(16),
        cost_estimate=cost(),
        name="last_step",
    )(start, weight, main, side, *others)


def merge_kernel(count, *refs):
    spreads, rows, owns = refs[:count], refs[count : 2 * count], refs[2 * count : 3 * count]
    other = refs[3 * count]
    for i in range(count):
        height, features = owns[i].shape
        which = spreads[i][...]
        for at, width in column_tiles(features):
            value = jnp.concatenate(
                [rows[i][e, :, at : at + width] for e in range(rows[i].shape[0])], axis=0
            )
            value = jnp.dot(which, value, preferred_element_type=F32)
            owns[i][:, at : at + width] = value[:height]
            other[i * height : (i + 1) * height, at : at + width] = value[height:].astype(BF16)


def merge_rows(spreads, rows):
    height, features = spreads[0].shape[0] // 2, rows[0].shape[2]
    count = len(rows)
    outs = [jax.ShapeDtypeStruct((height, features), F32)] * count
    outs.append(jax.ShapeDtypeStruct((count * height, features), BF16))
    arrays = [*spreads, *rows]
    return pl.pallas_call(
        functools.partial(merge_kernel, count),
        out_shape=outs,
        grid=(1,),
        in_specs=[whole(a) for a in arrays],
        out_specs=[whole(o) for o in outs],
        compiler_params=params(36),
        cost_estimate=cost(),
        name="merge_rows",
    )(*arrays)


def add_kernel(places, base, counts, joined, start, own, other, down, *refs):
    arrived, outs, total = refs[: sum(counts)], refs[sum(counts) : -1], refs[-1]
    features = own.shape[1]
    height = total.shape[0] // len(places)
    window = pl.ds(pl.multiple_of(start[0], LANES), down.shape[0])
    units = []
    for i, at in enumerate(places):
        mine = arrived[sum(counts[:i]) : sum(counts[: i + 1])]
        here = slice(i * height, (i + 1) * height)
        value = other[base + at : base + at + height, :].astype(F32)
        value = value + own[at : at + height, :]
        for a in mine:
            if a.shape[1] > features:
                value = value + a[:, :features].astype(F32)
        total[here, :] = value
        wide = mine[0].shape[1]
        units.append(mine[0][:, features:] if wide > features else mine[0][...])
    value = lax.dot_general(
        jnp.concatenate(units, axis=0),
        down[...],
        (((1,), (1,)), ((), ())),
        preferred_element_type=F32,
    )
    total[:, window] = total[:, window] + value
    if joined:
        outs[0][...] = total[...].astype(BF16)
    else:
        for i, out in enumerate(outs):
            out[:, :features] = total[i * height : (i + 1) * height, :].astype(BF16)
            out[:, features:] = units[i]


def add_step(start, term, down, places, arrived, joined=False):
    own, other, base = term
    features = own.shape[1]
    counts = [len(a) for a in arrived]
    height = arrived[0][0].shape[0]
    count = len(places)
    vmem = pl.BlockSpec(memory_space=pltpu.VMEM)
    if joined:
        outs = [jax.ShapeDtypeStruct((count * height, features), BF16)]
    else:
        shape = (height, features + down.shape[1])
        outs = [jax.ShapeDtypeStruct(shape, BF16)] * count
    return pl.pallas_call(
        functools.partial(add_kernel, places, base, counts, joined),
        out_shape=outs,
        in_specs=[pl.BlockSpec(memory_space=pltpu.SMEM)] + [vmem] * (3 + sum(counts)),
        out_specs=[vmem] * len(outs),
        scratch_shapes=[pltpu.VMEM((count * height, features), F32)],
        compiler_params=params(16),
        cost_estimate=cost(),
        name="add_step",
    )(start, own, other, down, *[a for b in arrived for a in b])


def window_width(count, size, total):
    need = max((i * size) % LANES + size for i in range(count))
    return min(total, -(-need // LANES) * LANES)


def on_device(
    tokens,
    route_ids,
    route_gates,
    expert_gate,
    expert_up,
    expert_down,
    shared_gate,
    shared_up,
    shared_down,
):
    n = lax.axis_size("expert")
    half = n // 2
    me = lax.axis_index("expert")
    row_count, features = tokens.shape
    top = route_ids.shape[1]
    experts = expert_gate.shape[0]
    slots = -(-4 * MOST // 16) * 16

    path = list(range(0, n, 2)) + list(range(n - 1, 0, -2))
    onward = [(path[i], path[(i + 1) % n]) for i in range(n)]
    backward = [(b, a) for a, b in onward]
    send_on = lambda a: lax.ppermute(a, "expert", onward)
    send_back = lambda a: lax.ppermute(a, "expert", backward)
    swap = lambda a: lax.ppermute(a, "tensor", [(0, 1), (1, 0)])

    first = (me * experts).reshape(1)

    size = shared_gate.shape[0]
    width = window_width(n, size, features)
    start = jnp.minimum(me * size // LANES * LANES, features - width)
    shift = (me * size - start).reshape(1)
    start = start.reshape(1)
    shifts = {i * size - min(i * size // LANES * LANES, features - width) for i in range(n)}
    weights = [f for w in (shared_gate, shared_up, shared_down.T) for f in (w, swap(w))]
    both, down, *sends = first_step(
        start, shift, sorted(shifts), tokens, route_ids.T, route_gates.T, weights, width
    )

    after = lambda x, y: lax.optimization_barrier((x, y))[0]
    split = row_count // 2
    tokens = sends[4]
    wide = tokens.shape[1]
    ahead, behind = [send_on(p) for p in sends[:2]], [send_back(p) for p in sends[2:4]]
    pick = lambda arrays, cut=0: pick_rows(first, arrays, experts, slots, top, cut)
    pairs, picked = {}, {}
    done = tokens
    for k in range(1, half):
        others = []
        for stream in (0, 1):
            full = (k < half - 1 or stream == 0, k < half - 1 or stream == 1)
            on, back = ahead[stream], behind[stream]
            if stream and k == 1:
                others = [tokens] + others
            sends = step_on(start, after(both, done), on, back, wide, full, others)
            done = sends[0]
            ahead[stream], behind[stream] = send_on(sends[0]), send_back(sends[1])
            others = [on, back]
            if stream == 0 and k > 1:
                picked[k - 1] = pick([after(pairs[k - 1][0], done), pairs[k - 1][1]], -row_count if k == 2 else 0)
                done = picked[k - 1][1]
        pairs[k] = [sends[2], swap(sends[2])]
    main = [ahead[0], behind[1]]
    [upper] = last_step(start, after(both, done), main[0], behind[0], wide)
    k = half - 1
    picked[k] = pick([after(pairs[k][0], upper), pairs[k][1]])
    done = picked[k][1]
    lower, end = last_step(start, after(both, done), main[1], ahead[1], wide, main[:1])
    units = upper, lower
    picked[0] = pick([pairs[1][0], end, pairs[1][1], swap(end)], row_count)

    lag = send_on(units[1]), send_back(units[0])
    routed = {}
    for at in range(0, half, 4):
        group = list(range(at, min(at + 4, half)))
        rows = [picked[j][0] for j in group]
        weights = expert_gate, expert_up, expert_down
        routed.update(zip(group, run_experts(first, rows, *weights, top)))

    def terms_of(chunks, done):
        spreads = [picked[c][1] for c in chunks]
        spreads[0] = after(spreads[0], done)
        *owns, other = merge_rows(spreads, [routed[c] for c in chunks])
        other = swap(other)
        return {c: (own, other, i * block) for i, (c, own) in enumerate(zip(chunks, owns))}

    block = 2 * row_count
    terms = terms_of([0, half - 1], lag)
    lead = add_step(
        start, terms[0], down, (row_count, row_count + split), [[units[0]], [units[1]]]
    )
    done = lead[0]
    lead = send_on(lead[0]), send_back(lead[1])
    for k in range(half - 1, 0, -1):
        lag = add_step(start, terms[k], after(down, done), (3 * split, 0), [[lag[0]], [lag[1]]])
        done = lag[0]
        lag = send_on(lag[0]), send_back(lag[1])
        if k > 1 and k - 1 not in terms:
            terms.update(terms_of([k - 1, k - 2] if k > 2 else [k - 1], done))
            done = terms[k - 1][1]
        lead = add_step(
            start, terms[k], after(down, done), (split, 2 * split), [[lead[0]], [lead[1]]]
        )
        done = lead[0]
        lead = send_on(lead[0]), send_back(lead[1])
    arrived = [[lead[0], lag[1]], [lag[0], lead[1]]]
    return add_step(start, terms[0], after(down, done), (0, split), arrived, joined=True)[0]


def solution(mesh):
    in_specs = (
        P(("group", "expert", "tensor"), None),
        P(("group", "expert", "tensor"), None),
        P(("group", "expert", "tensor"), None),
        P("expert", None, "tensor"),
        P("expert", None, "tensor"),
        P("expert", "tensor", None),
        P("expert", "tensor"),
        P("expert", "tensor"),
        P("tensor", "expert"),
    )
    out_specs = P(("group", "expert", "tensor"), None)
    return jax.shard_map(
        on_device, mesh=mesh, in_specs=in_specs, out_specs=out_specs, check_vma=False
    )
```

```python
import functools

import jax
import jax.numpy as jnp
from jax import lax
from jax.experimental import pallas as pl
from jax.experimental.pallas import tpu as pltpu
from jax.sharding import PartitionSpec as P

MOST = 18
LANES = 128
MIB = 1 << 20
BF16 = jnp.bfloat16
F32 = jnp.float32


def cost(flops):
    return pl.CostEstimate(flops=flops, bytes_accessed=1000, transcendentals=0)


def params(mib):
    return pltpu.CompilerParams(vmem_limit_bytes=mib * MIB)


def column_tiles(total, width=512):
    return [(at, min(width, total - at)) for at in range(0, total, width)]


def silu(value):
    return value * (1.0 / (1.0 + jnp.exp(-value)))


def whole(array):
    return pl.BlockSpec(array.shape, lambda i: (0,) * array.ndim)


def pick_kernel(count, experts, top, first, *refs):
    tokens, out, spread = refs[:count], refs[count], refs[count + 1]
    features = out.shape[2]
    height, slots = spread.shape
    notes = jnp.concatenate([t[:, features - LANES :] for t in tokens], axis=0).astype(F32)
    lane = lax.broadcasted_iota(jnp.int32, notes.shape, 1)
    named = jnp.zeros(notes.shape, F32)
    for e in range(experts):
        same = (notes == (first[0] + e).astype(F32)) & (lane < top)
        hit = jnp.max(jnp.where(same, 1.0, 0.0), axis=1, keepdims=True)
        named = jnp.where(lane == e, hit, named)
    down = lax.broadcasted_iota(jnp.int32, (height, height), 0)
    across = lax.broadcasted_iota(jnp.int32, (height, height), 1)
    upto = jnp.where(across <= down, 1.0, 0.0).astype(BF16)
    rank = jnp.dot(upto, named.astype(BF16), preferred_element_type=F32).astype(jnp.int32) - 1
    slot = jnp.where(named > 0.0, rank + lane * (slots // experts), -1)
    turned = jnp.transpose(slot.astype(F32)).astype(jnp.int32)
    number = lax.broadcasted_iota(jnp.int32, (slots, height), 0)
    column = lax.broadcasted_iota(jnp.int32, (height, slots), 1)
    picks = number == turned[0:1, :]
    back = column == slot[:, 0:1]
    for e in range(1, experts):
        picks = picks | (number == turned[e : e + 1, :])
        back = back | (column == slot[:, e : e + 1])
    picks = jnp.where(picks, 1.0, 0.0).astype(BF16)
    spread[...] = jnp.where(back, 1.0, 0.0).astype(BF16)
    for at, width in column_tiles(features):
        piece = jnp.concatenate([t[:, at : at + width] for t in tokens], axis=0)
        rows = jnp.dot(picks, piece, preferred_element_type=F32).astype(BF16)
        out[:, :, at : at + width] = rows.reshape(experts, slots // experts, width)


def pick_rows(first, tokens, experts, slots, top, work):
    height = sum(t.shape[0] for t in tokens)
    features = tokens[0].shape[1]
    vmem = pl.BlockSpec(memory_space=pltpu.VMEM)
    return pl.pallas_call(
        functools.partial(pick_kernel, len(tokens), experts, top),
        out_shape=[
            jax.ShapeDtypeStruct((experts, slots, features), BF16),
            jax.ShapeDtypeStruct((height, experts * slots), BF16),
        ],
        in_specs=[pl.BlockSpec(memory_space=pltpu.SMEM)] + [vmem] * len(tokens),
        out_specs=[vmem, vmem],
        compiler_params=params(16),
        cost_estimate=cost(work),
        name="pick_rows",
    )(first, *tokens)


def expert_kernel(count, top, first, *refs):
    rows_in, (gate, up, down) = refs[:count], refs[count : count + 3]
    rows_out, rows = refs[count + 3 : 2 * count + 3], refs[2 * count + 3]
    slots, wide = rows_in[0].shape[1:]
    features = down.shape[2]
    for i, r in enumerate(rows_in):
        rows[i * slots : (i + 1) * slots, :] = r[0]
    notes = rows[:, features:].astype(F32)
    lane = lax.broadcasted_iota(jnp.int32, notes.shape, 1)
    expert = (first[0] + pl.program_id(0)).astype(F32)
    chosen = jnp.where((notes == expert) & (lane < top), 1.0, 0.0)
    scale = jnp.zeros((notes.shape[0], 1), F32)
    for part in (1, 2, 3):
        moved = jnp.concatenate([notes[:, part * top :], notes[:, : part * top]], axis=1)
        scale = scale + jnp.sum(chosen * moved, axis=1, keepdims=True)
    value = rows[:, :features]
    gated = jnp.dot(value, gate[0], preferred_element_type=F32)
    upward = jnp.dot(value, up[0], preferred_element_type=F32)
    hidden = (silu(gated) * upward * scale).astype(BF16)
    for at, width in column_tiles(features):
        done = jnp.dot(hidden, down[0, :, at : at + width], preferred_element_type=F32)
        done = done.astype(BF16)
        for i, r in enumerate(rows_out):
            r[0, :, at : at + width] = done[i * slots : (i + 1) * slots]


def run_experts(first, rows, gate, up, down, top):
    experts, slots, wide = rows[0].shape
    features, hidden = gate.shape[1:]
    count = len(rows)
    height = count * slots
    return pl.pallas_call(
        functools.partial(expert_kernel, count, top),
        out_shape=[jax.ShapeDtypeStruct((experts, slots, features), BF16)] * count,
        grid=(experts,),
        in_specs=[pl.BlockSpec(memory_space=pltpu.SMEM)]
        + [pl.BlockSpec((1, slots, wide), lambda e: (e, 0, 0))] * count
        + [
            pl.BlockSpec((1, features, hidden), lambda e: (e, 0, 0)),
            pl.BlockSpec((1, features, hidden), lambda e: (e, 0, 0)),
            pl.BlockSpec((1, hidden, features), lambda e: (e, 0, 0)),
        ],
        out_specs=[pl.BlockSpec((1, slots, features), lambda e: (e, 0, 0))] * count,
        scratch_shapes=[pltpu.VMEM((height, wide), BF16)],
        compiler_params=params(38),
        cost_estimate=cost(100000000000),
        name="run_experts",
    )(first, *rows, gate, up, down)


def note_kernel(tokens, ids, gates, *sends):
    rows, features = tokens.shape
    gate = gates[...]
    high = gate.astype(BF16).astype(F32)
    middle = (gate - high).astype(BF16).astype(F32)
    low = gate - high - middle
    notes = [ids[...].astype(F32), high, middle, low]
    notes.append(jnp.zeros((LANES - 4 * ids.shape[0], rows), F32))
    notes = jnp.transpose(jnp.concatenate(notes, axis=0)).astype(BF16)
    split = rows // 2
    for i, out in enumerate(sends):
        here = slice(i * split, (i + 1) * split) if i < 2 else slice(0, rows)
        out[:, :features] = tokens[here, :]
        out[:, features:] = notes[here]


def note_tokens(tokens, ids, gates):
    rows, wide = tokens.shape[0], tokens.shape[1] + LANES
    outs = [jax.ShapeDtypeStruct((r, wide), BF16) for r in (rows // 2, rows // 2, rows)]
    return pl.pallas_call(
        note_kernel,
        out_shape=outs,
        grid=(1,),
        in_specs=[whole(a) for a in (tokens, ids, gates)],
        out_specs=[whole(o) for o in outs],
        compiler_params=params(60),
        cost_estimate=cost(1000),
        name="note_tokens",
    )(tokens, ids, gates)


def first_kernel(shifts, start, shift, tokens, *refs):
    parts, (weight, down, sums) = refs[:6], refs[6:]
    height, width = parts[0].shape
    gap = weight.shape[0] - height
    for s in shifts:

        @pl.when(shift[0] == s)
        def _():
            for part, out, at in zip(parts, [weight] * 4 + [down] * 2, (0, 1, 2, 3, 0, 1)):
                size = part.shape[1]
                here = slice(at * size, (at + 1) * size)
                if s:
                    out[:s, here] = jnp.zeros((s, size), BF16)
                out[s : s + height, here] = part[...]
                if s < gap:
                    out[s + height :, here] = jnp.zeros((gap - s, size), BF16)

    window = pl.ds(pl.multiple_of(start[0], LANES), weight.shape[0])
    value = jnp.dot(tokens[:, window], weight[...], preferred_element_type=F32)
    sums[...] = value.astype(BF16)


def first_step(start, shift, shifts, tokens, weights, width):
    inner = weights[0].shape[1]
    outs = [(width, 4 * inner), (width, 2 * inner), (tokens.shape[0], 4 * inner)]
    outs = [jax.ShapeDtypeStruct(shape, BF16) for shape in outs]
    smem = pl.BlockSpec(memory_space=pltpu.SMEM)
    arrays = [tokens, *weights]
    return pl.pallas_call(
        functools.partial(first_kernel, shifts),
        out_shape=outs,
        grid=(1,),
        in_specs=[smem, smem] + [whole(a) for a in arrays],
        out_specs=[whole(o) for o in outs],
        compiler_params=params(60),
        cost_estimate=cost(100000000000),
        name="first_step",
    )(start, shift, *arrays)


def step_kernel(wide, sends, start, weight, on, back, *refs):
    others, outs = (refs[:-3], refs[-3:]) if len(refs) > 2 else ((), refs)
    height = on.shape[0]
    window = pl.ds(pl.multiple_of(start[0], LANES), weight.shape[0])
    piece = jnp.concatenate([on[:, window], back[:, window]], axis=0)
    value = jnp.dot(piece, weight[...], preferred_element_type=F32)
    for i, arrived in enumerate((on, back)):
        part = value[i * height : (i + 1) * height] + arrived[:, wide:].astype(F32)
        if sends[i]:
            outs[i][:, :wide] = arrived[:, :wide]
            outs[i][:, wide:] = part.astype(BF16)
        else:
            outs[i][...] = part.astype(BF16)
    if others:
        at = 0
        for r in (*others, on, back):
            outs[2][at : at + r.shape[0], :] = r[:, :wide]
            at += r.shape[0]


def step_on(start, weight, on, back, wide, sends, others):
    height, width = on.shape[0], weight.shape[1]
    vmem = pl.BlockSpec(memory_space=pltpu.VMEM)
    shapes = [(height, wide + width) if full else (height, width) for full in sends]
    if others:
        shapes.append((sum(o.shape[0] for o in others) + 2 * height, wide))
    return pl.pallas_call(
        functools.partial(step_kernel, wide, sends),
        out_shape=[jax.ShapeDtypeStruct(shape, BF16) for shape in shapes],
        in_specs=[pl.BlockSpec(memory_space=pltpu.SMEM)] + [vmem] * (3 + len(others)),
        out_specs=[vmem] * len(shapes),
        compiler_params=params(16),
        cost_estimate=cost(10000000000),
        name="step_on",
    )(start, weight, on, back, *others)


def open_kernel(start, weight, *refs):
    on, back, terms, outs = refs[:2], refs[2:4], refs[4], refs[5:]
    pair = outs[2]
    height, wide = on[0].shape
    window = pl.ds(pl.multiple_of(start[0], LANES), weight.shape[0])
    piece = jnp.concatenate([r[:, window] for r in (*on, *back)], axis=0)
    value = jnp.dot(piece, weight[...], preferred_element_type=F32)
    terms[...] = value[: 2 * height]
    for i, r in enumerate(back):
        outs[i][:, :wide] = r[...]
        outs[i][:, wide:] = value[(2 + i) * height : (3 + i) * height].astype(BF16)
    for i, r in enumerate((on[0], back[0], on[1], back[1])):
        pair[i * height : (i + 1) * height, :] = r[...]


def open_step(start, weight, on, back):
    height, wide = on[0].shape
    width = weight.shape[1]
    outs = [jax.ShapeDtypeStruct((2 * height, width), F32)]
    outs += [jax.ShapeDtypeStruct((height, wide + width), BF16)] * 2
    outs += [jax.ShapeDtypeStruct((4 * height, wide), BF16)]
    vmem = pl.BlockSpec(memory_space=pltpu.VMEM)
    return pl.pallas_call(
        open_kernel,
        out_shape=outs,
        in_specs=[pl.BlockSpec(memory_space=pltpu.SMEM)] + [vmem] * 5,
        out_specs=[vmem] * 4,
        compiler_params=params(16),
        cost_estimate=cost(100000000000),
        name="open_step",
    )(start, weight, *on, *back)


def onward_kernel(terms, sums, *refs):
    on, outs = refs[:2], refs[2:]
    height, wide = on[0].shape
    for i, r in enumerate(on):
        here = slice(i * height, (i + 1) * height)
        outs[i][:, :wide] = r[...]
        outs[i][:, wide:] = (terms[here, :] + sums[here, :].astype(F32)).astype(BF16)


def onward_step(terms, sums, on):
    height, wide = on[0].shape
    vmem = pl.BlockSpec(memory_space=pltpu.VMEM)
    out = jax.ShapeDtypeStruct((height, wide + sums.shape[1]), BF16)
    return pl.pallas_call(
        onward_kernel,
        out_shape=[out] * 2,
        in_specs=[vmem] * 4,
        out_specs=[vmem] * 2,
        compiler_params=params(16),
        cost_estimate=cost(10000000000),
        name="onward_step",
    )(terms, sums, *on)


def last_kernel(wide, start, weight, main, side, *refs):
    others, (units, *tokens) = (refs[:1], refs[1:]) if len(refs) == 3 else ((), refs)
    height = main.shape[0]
    window = pl.ds(pl.multiple_of(start[0], LANES), weight.shape[0])
    value = jnp.dot(main[:, window], weight[...], preferred_element_type=F32)
    value = value + main[:, wide:].astype(F32) + side[...].astype(F32)
    half = value.shape[1] // 2
    units[...] = (silu(value[:, :half]) * value[:, half:]).astype(BF16)
    if others:
        for i, r in enumerate((*others, main)):
            tokens[0][i * height : (i + 1) * height, :] = r[:, :wide]


def last_step(start, weight, main, side, wide, others=()):
    height = main.shape[0]
    vmem = pl.BlockSpec(memory_space=pltpu.VMEM)
    return pl.pallas_call(
        functools.partial(last_kernel, wide),
        out_shape=[jax.ShapeDtypeStruct((height, weight.shape[1] // 2), BF16)]
        + [jax.ShapeDtypeStruct((2 * height, wide), BF16)] * len(others),
        in_specs=[pl.BlockSpec(memory_space=pltpu.SMEM)] + [vmem] * (3 + len(others)),
        out_specs=[vmem] * (1 + len(others)),
        compiler_params=params(16),
        cost_estimate=cost(7000000000),
        name="last_step",
    )(start, weight, main, side, *others)


def merge_kernel(count, *refs):
    spreads, rows, owns = refs[:count], refs[count : 2 * count], refs[2 * count : 3 * count]
    other = refs[3 * count]
    for i in range(count):
        height, features = owns[i].shape
        which = spreads[i][...]
        for at, width in column_tiles(features):
            value = jnp.concatenate(
                [rows[i][e, :, at : at + width] for e in range(rows[i].shape[0])], axis=0
            )
            value = jnp.dot(which, value, preferred_element_type=F32)
            owns[i][:, at : at + width] = value[:height]
            other[i * height : (i + 1) * height, at : at + width] = value[height:].astype(BF16)


def merge_rows(spreads, rows):
    height, features = spreads[0].shape[0] // 2, rows[0].shape[2]
    count = len(rows)
    outs = [jax.ShapeDtypeStruct((height, features), F32)] * count
    outs.append(jax.ShapeDtypeStruct((count * height, features), BF16))
    arrays = [*spreads, *rows]
    return pl.pallas_call(
        functools.partial(merge_kernel, count),
        out_shape=outs,
        grid=(1,),
        in_specs=[whole(a) for a in arrays],
        out_specs=[whole(o) for o in outs],
        compiler_params=params(36),
        cost_estimate=cost(100000000000),
        name="merge_rows",
    )(*arrays)


def add_kernel(places, base, counts, joined, narrow, start, own, other, down, *refs):
    arrived, outs, total = refs[: sum(counts)], refs[sum(counts) : -1], refs[-1]
    features = own.shape[1]
    height = total.shape[0] // len(places)
    window = pl.ds(pl.multiple_of(start[0], LANES), down.shape[0])
    units = []
    for i, at in enumerate(places):
        mine = arrived[sum(counts[:i]) : sum(counts[: i + 1])]
        here = slice(i * height, (i + 1) * height)
        value = other[base + at : base + at + height, :].astype(F32)
        value = value + own[at : at + height, :]
        for a in mine:
            if a.shape[1] > features:
                value = value + a[:, :features].astype(F32)
        total[here, :] = value
        wide = mine[0].shape[1]
        units.append(mine[0][:, features:] if wide > features else mine[0][...])
    value = lax.dot_general(
        jnp.concatenate(units, axis=0),
        down[...],
        (((1,), (1,)), ((), ())),
        preferred_element_type=F32,
    )
    total[:, window] = total[:, window] + value
    if joined:
        outs[0][...] = total[...]
    else:
        for i, out in enumerate(outs):
            out[:, :features] = total[i * height : (i + 1) * height, :].astype(BF16)
            if not narrow:
                out[:, features:] = units[i]


def add_step(start, term, down, places, arrived, joined=False, narrow=False):
    own, other, base = term
    features = own.shape[1]
    counts = [len(a) for a in arrived]
    height = arrived[0][0].shape[0]
    count = len(places)
    vmem = pl.BlockSpec(memory_space=pltpu.VMEM)
    if joined:
        outs = [jax.ShapeDtypeStruct((count * height, features), F32)]
    else:
        shape = (height, features + (0 if narrow else down.shape[1]))
        outs = [jax.ShapeDtypeStruct(shape, BF16)] * count
    return pl.pallas_call(
        functools.partial(add_kernel, places, base, counts, joined, narrow),
        out_shape=outs,
        in_specs=[pl.BlockSpec(memory_space=pltpu.SMEM)] + [vmem] * (3 + sum(counts)),
        out_specs=[vmem] * len(outs),
        scratch_shapes=[pltpu.VMEM((count * height, features), F32)],
        compiler_params=params(16),
        cost_estimate=cost(100000000000),
        name="add_step",
    )(start, own, other, down, *[a for b in arrived for a in b])


def join_kernel(sums, first, second, out):
    height, features = first.shape[0], out.shape[1]
    for i, r in enumerate((first, second)):
        here = slice(i * height, (i + 1) * height)
        out[here, :] = (sums[here, :] + r[:, :features].astype(F32)).astype(BF16)


def join(sums, arrived):
    vmem = pl.BlockSpec(memory_space=pltpu.VMEM)
    return pl.pallas_call(
        join_kernel,
        out_shape=jax.ShapeDtypeStruct(sums.shape, BF16),
        in_specs=[vmem] * 3,
        out_specs=vmem,
        compiler_params=params(16),
        cost_estimate=cost(100000000000),
        name="join",
    )(sums, *arrived)


def window_width(count, size, total):
    need = max((i * size) % LANES + size for i in range(count))
    return min(total, -(-need // LANES) * LANES)


def on_device(
    tokens,
    route_ids,
    route_gates,
    expert_gate,
    expert_up,
    expert_down,
    shared_gate,
    shared_up,
    shared_down,
):
    n = lax.axis_size("expert")
    half = n // 2
    me = lax.axis_index("expert")
    row_count, features = tokens.shape
    top = route_ids.shape[1]
    experts = expert_gate.shape[0]
    slots = -(-4 * MOST // 16) * 16

    path = list(range(0, n, 2)) + list(range(n - 1, 0, -2))
    onward = [(path[i], path[(i + 1) % n]) for i in range(n)]
    backward = [(b, a) for a, b in onward]
    send_on = lambda a: lax.ppermute(a, "expert", onward)
    send_back = lambda a: lax.ppermute(a, "expert", backward)
    swap = lambda a: lax.ppermute(a, "tensor", [(0, 1), (1, 0)])

    first = (me * experts).reshape(1)

    size = shared_gate.shape[0]
    width = window_width(n, size, features)
    start = jnp.minimum(me * size // LANES * LANES, features - width)
    shift = (me * size - start).reshape(1)
    start = start.reshape(1)
    shifts = {i * size - min(i * size // LANES * LANES, features - width) for i in range(n)}
    weights = [f for w in (shared_gate, shared_up, shared_down.T) for f in (w, swap(w))]
    after = lambda x, y: lax.optimization_barrier((x, y))[0]
    split = row_count // 2
    *parts, tokens = note_tokens(tokens, route_ids.T, route_gates.T)
    wide = tokens.shape[1]
    ahead, behind = [send_on(p) for p in parts], [send_back(p) for p in parts]
    own = swap(tokens)
    first_start = after(start, own)
    both, down, sums = first_step(first_start, shift, sorted(shifts), tokens, weights, width)
    sums = send_on(sums)
    pick = lambda arrays, work=10000000000: pick_rows(first, arrays, experts, slots, top, work)
    pairs, picked = {}, {}
    terms, *sends, pair = open_step(after(start, down), both, ahead, behind)
    pairs[1] = [pair, swap(pair)]
    behind = [send_back(m) for m in sends]
    sends = onward_step(terms, sums, ahead)
    ahead = [send_on(m) for m in sends]
    done = sends[0]
    for k in range(2, half):
        others = []
        for stream in (0, 1):
            full = (k < half - 1 or stream == 0, k < half - 1 or stream == 1)
            on, back = ahead[stream], behind[stream]
            sends = step_on(after(start, done), both, on, back, wide, full, others)
            done = sends[0]
            ahead[stream], behind[stream] = send_on(sends[0]), send_back(sends[1])
            others = [on, back]
            if stream == 0:
                picked[k - 1] = pick([after(pairs[k - 1][0], done), pairs[k - 1][1]])
                done = picked[k - 1][1]
        pairs[k] = [sends[2], swap(sends[2])]
    main = [ahead[0], behind[1]]
    [upper] = last_step(after(start, done), both, main[0], behind[0], wide)
    k = half - 1
    picked[k] = pick([after(pairs[k][0], upper), pairs[k][1]], work=1000)
    done = picked[k][1]
    lower, end = last_step(after(start, done), both, main[1], ahead[1], wide, main[:1])
    units = upper, lower
    picked[0] = pick([tokens, end, own, swap(end)])

    lag = send_on(units[1]), send_back(units[0])
    routed = {}
    for at in range(0, half, 4):
        group = list(range(at, min(at + 4, half)))
        rows = [picked[j][0] for j in group]
        weights = expert_gate, expert_up, expert_down
        routed.update(zip(group, run_experts(first, rows, *weights, top)))

    def terms_of(chunks, done):
        spreads = [picked[c][1] for c in chunks]
        spreads[0] = after(spreads[0], done)
        *owns, other = merge_rows(spreads, [routed[c] for c in chunks])
        other = swap(other)
        return {c: (own, other, i * block) for i, (c, own) in enumerate(zip(chunks, owns))}

    block = 2 * row_count
    terms = terms_of([0], lag)
    terms.update(terms_of([half - 1], terms[0][0]))
    places, done = (row_count, row_count + split), terms[half - 1][0]
    lead = add_step(after(start, done), terms[0], down, places, [[units[0]], [units[1]]])
    done = lead[0]
    lead = send_on(lead[0]), send_back(lead[1])
    for k in range(half - 1, 0, -1):
        lag = add_step(after(start, done), terms[k], down, (3 * split, 0), [[lag[0]], [lag[1]]])
        done = lag[0]
        lag = send_on(lag[0]), send_back(lag[1])
        if k > 1 and k - 1 not in terms:
            terms.update(terms_of([k - 1, k - 2] if k > 2 else [k - 1], done))
            done = terms[k - 1][0]
        places, arrived = (split, 2 * split), [[lead[0]], [lead[1]]]
        lead = add_step(after(start, done), terms[k], down, places, arrived, narrow=k == 1)
        done = lead[0]
        lead = send_on(lead[0]), send_back(lead[1])
    arrived = [[lag[1]], [lag[0]]]
    [sums] = add_step(after(start, done), terms[0], down, (0, split), arrived, joined=True)
    return join(sums, lead)


def solution(mesh):
    in_specs = (
        P(("group", "expert", "tensor"), None),
        P(("group", "expert", "tensor"), None),
        P(("group", "expert", "tensor"), None),
        P("expert", None, "tensor"),
        P("expert", None, "tensor"),
        P("expert", "tensor", None),
        P("expert", "tensor"),
        P("expert", "tensor"),
        P("tensor", "expert"),
    )
    out_specs = P(("group", "expert", "tensor"), None)
    return jax.shard_map(
        on_device, mesh=mesh, in_specs=in_specs, out_specs=out_specs, check_vma=False
    )
```

```python
import functools

import jax
import jax.numpy as jnp
from jax import lax
from jax.experimental import pallas as pl
from jax.experimental.pallas import tpu as pltpu
from jax.sharding import PartitionSpec as P

MOST = 18
LANES = 128
MIB = 1 << 20
BF16 = jnp.bfloat16
F32 = jnp.float32


def cost(flops):
    return pl.CostEstimate(flops=flops, bytes_accessed=1000, transcendentals=0)


def params(mib):
    return pltpu.CompilerParams(vmem_limit_bytes=mib * MIB)


def column_tiles(total, width=512):
    return [(at, min(width, total - at)) for at in range(0, total, width)]


def silu(value):
    return value * (1.0 / (1.0 + jnp.exp(-value)))


def whole(array):
    return pl.BlockSpec(array.shape, lambda i: (0,) * array.ndim)


def pick_kernel(count, experts, top, first, *refs):
    tokens, out, spread = refs[:count], refs[count], refs[count + 1]
    features = out.shape[2]
    height, slots = spread.shape
    notes = jnp.concatenate([t[:, features - LANES :] for t in tokens], axis=0).astype(F32)
    lane = lax.broadcasted_iota(jnp.int32, notes.shape, 1)
    named = jnp.zeros(notes.shape, F32)
    for e in range(experts):
        same = (notes == (first[0] + e).astype(F32)) & (lane < top)
        hit = jnp.max(jnp.where(same, 1.0, 0.0), axis=1, keepdims=True)
        named = jnp.where(lane == e, hit, named)
    down = lax.broadcasted_iota(jnp.int32, (height, height), 0)
    across = lax.broadcasted_iota(jnp.int32, (height, height), 1)
    upto = jnp.where(across <= down, 1.0, 0.0).astype(BF16)
    rank = jnp.dot(upto, named.astype(BF16), preferred_element_type=F32).astype(jnp.int32) - 1
    slot = jnp.where(named > 0.0, rank + lane * (slots // experts), -1)
    turned = jnp.transpose(slot.astype(F32)).astype(jnp.int32)
    number = lax.broadcasted_iota(jnp.int32, (slots, height), 0)
    column = lax.broadcasted_iota(jnp.int32, (height, slots), 1)
    picks = number == turned[0:1, :]
    back = column == slot[:, 0:1]
    for e in range(1, experts):
        picks = picks | (number == turned[e : e + 1, :])
        back = back | (column == slot[:, e : e + 1])
    picks = jnp.where(picks, 1.0, 0.0).astype(BF16)
    spread[...] = jnp.where(back, 1.0, 0.0).astype(BF16)
    for at, width in column_tiles(features):
        piece = jnp.concatenate([t[:, at : at + width] for t in tokens], axis=0)
        rows = jnp.dot(picks, piece, preferred_element_type=F32).astype(BF16)
        out[:, :, at : at + width] = rows.reshape(experts, slots // experts, width)


def pick_rows(first, tokens, experts, slots, top, work):
    height = sum(t.shape[0] for t in tokens)
    features = tokens[0].shape[1]
    vmem = pl.BlockSpec(memory_space=pltpu.VMEM)
    return pl.pallas_call(
        functools.partial(pick_kernel, len(tokens), experts, top),
        out_shape=[
            jax.ShapeDtypeStruct((experts, slots, features), BF16),
            jax.ShapeDtypeStruct((height, experts * slots), BF16),
        ],
        in_specs=[pl.BlockSpec(memory_space=pltpu.SMEM)] + [vmem] * len(tokens),
        out_specs=[vmem, vmem],
        compiler_params=params(16),
        cost_estimate=cost(work),
        name="pick_rows",
    )(first, *tokens)


def expert_kernel(count, pieces, top, first, *refs):
    rows_in, weights = refs[:count], refs[count : count + 3]
    rows_out, refs = refs[count + 3 : 2 * count + 3], refs[2 * count + 3 :]
    rows, held, sems, piece_sems = refs[0], refs[1:4], refs[4], refs[5]
    slots, wide = rows_in[0].shape[1:]
    features = held[0].shape[1]
    here = pl.program_id(0)
    last = pl.num_programs(0) - 1
    depth = features // pieces

    def fetch(expert, which):
        slot = lax.rem(expert, 2)
        copy = pltpu.make_async_copy
        return copy(weights[which].at[expert], held[which].at[slot], sems.at[slot, which])

    def fetch_piece(at, which):
        part = pl.ds(at * depth, depth)
        copy = pltpu.make_async_copy
        return copy(weights[which].at[0, part], held[which].at[0, part], piece_sems.at[at, which])

    @pl.when(here == 0)
    def _():
        for at in range(pieces):
            for which in range(2):
                fetch_piece(at, which).start()
        fetch(0, 2).start()

    for i, r in enumerate(rows_in):
        rows[i * slots : (i + 1) * slots, :] = r[here]
    notes = rows[:, features:].astype(F32)
    lane = lax.broadcasted_iota(jnp.int32, notes.shape, 1)
    expert = (first[0] + here).astype(F32)
    chosen = jnp.where((notes == expert) & (lane < top), 1.0, 0.0)
    scale = jnp.zeros((notes.shape[0], 1), F32)
    for part in (1, 2, 3):
        moved = jnp.concatenate([notes[:, part * top :], notes[:, : part * top]], axis=1)
        scale = scale + jnp.sum(chosen * moved, axis=1, keepdims=True)

    def finish(gated, upward, down):
        hidden = (silu(gated) * upward * scale).astype(BF16)
        for at, width in column_tiles(features):
            done = jnp.dot(hidden, down[:, at : at + width], preferred_element_type=F32)
            done = done.astype(BF16)
            for i, r in enumerate(rows_out):
                r[here, :, at : at + width] = done[i * slots : (i + 1) * slots]

    @pl.when(here == 0)
    def _():
        gated = upward = None
        for at in range(pieces):
            for which in range(2):
                fetch_piece(at, which).wait()
            if at == 1:

                @pl.when(here < last)
                def _():
                    for which in range(3):
                        fetch(1, which).start()

            part = slice(at * depth, (at + 1) * depth)
            value = rows[:, part]
            g = jnp.dot(value, held[0][0, part], preferred_element_type=F32)
            u = jnp.dot(value, held[1][0, part], preferred_element_type=F32)
            gated, upward = (g, u) if at == 0 else (gated + g, upward + u)

        fetch(0, 2).wait()
        finish(gated, upward, held[2].at[0])

    @pl.when(here > 0)
    def _():
        @pl.when(here < last)
        def _():
            for which in range(3):
                fetch(here + 1, which).start()

        slot = lax.rem(here, 2)
        for which in range(2):
            fetch(here, which).wait()
        value = rows[:, :features]
        gated = jnp.dot(value, held[0][slot], preferred_element_type=F32)
        upward = jnp.dot(value, held[1][slot], preferred_element_type=F32)
        fetch(here, 2).wait()
        finish(gated, upward, held[2].at[slot])


def run_experts(first, rows, gate, up, down, top):
    experts, slots, wide = rows[0].shape
    features, hidden = gate.shape[1:]
    count = len(rows)
    height = count * slots
    pieces = 7
    vmem = pl.BlockSpec(memory_space=pltpu.VMEM)
    rows = [pltpu.with_memory_space_constraint(r, pltpu.VMEM) for r in rows]
    weights = [pltpu.with_memory_space_constraint(w, pltpu.HBM) for w in (gate, up, down)]
    return pl.pallas_call(
        functools.partial(expert_kernel, count, pieces, top),
        out_shape=[pltpu.VMEM((experts, slots, features), BF16)] * count,
        grid=(experts,),
        in_specs=[pl.BlockSpec(memory_space=pltpu.SMEM)]
        + [vmem] * count
        + [pl.BlockSpec(memory_space=pl.ANY)] * 3,
        out_specs=[vmem] * count,
        scratch_shapes=[pltpu.VMEM((height, wide), BF16)]
        + [pltpu.VMEM((2, *w.shape[1:]), BF16) for w in (gate, up, down)]
        + [pltpu.SemaphoreType.DMA((2, 3)), pltpu.SemaphoreType.DMA((pieces, 2))],
        compiler_params=params(28),
        cost_estimate=cost(100000000000),
        name="run_experts",
    )(first, *rows, *weights)


def note_kernel(tokens, ids, gates, *sends):
    rows, features = tokens.shape
    gate = gates[...]
    high = gate.astype(BF16).astype(F32)
    middle = (gate - high).astype(BF16).astype(F32)
    low = gate - high - middle
    notes = [ids[...].astype(F32), high, middle, low]
    notes.append(jnp.zeros((LANES - 4 * ids.shape[0], rows), F32))
    notes = jnp.transpose(jnp.concatenate(notes, axis=0)).astype(BF16)
    split = rows // 2
    for i, out in enumerate(sends):
        here = slice(i * split, (i + 1) * split) if i < 2 else slice(0, rows)
        out[:, :features] = tokens[here, :]
        out[:, features:] = notes[here]


def note_tokens(tokens, ids, gates):
    rows, wide = tokens.shape[0], tokens.shape[1] + LANES
    outs = [jax.ShapeDtypeStruct((r, wide), BF16) for r in (rows // 2, rows // 2, rows)]
    return pl.pallas_call(
        note_kernel,
        out_shape=outs,
        grid=(1,),
        in_specs=[whole(a) for a in (tokens, ids, gates)],
        out_specs=[whole(o) for o in outs],
        compiler_params=params(60),
        cost_estimate=cost(1000),
        name="note_tokens",
    )(tokens, ids, gates)


def first_kernel(shifts, start, shift, tokens, *refs):
    parts, (weight, down, sums) = refs[:6], refs[6:]
    height, width = parts[0].shape
    gap = weight.shape[0] - height
    for s in shifts:

        @pl.when(shift[0] == s)
        def _():
            for part, out, at in zip(parts, [weight] * 4 + [down] * 2, (0, 1, 2, 3, 0, 1)):
                size = part.shape[1]
                here = slice(at * size, (at + 1) * size)
                if s:
                    out[:s, here] = jnp.zeros((s, size), BF16)
                out[s : s + height, here] = part[...]
                if s < gap:
                    out[s + height :, here] = jnp.zeros((gap - s, size), BF16)

    window = pl.ds(pl.multiple_of(start[0], LANES), weight.shape[0])
    value = jnp.dot(tokens[:, window], weight[...], preferred_element_type=F32)
    sums[...] = value.astype(BF16)


def first_step(start, shift, shifts, tokens, weights, width):
    inner = weights[0].shape[1]
    outs = [(width, 4 * inner), (width, 2 * inner), (tokens.shape[0], 4 * inner)]
    outs = [jax.ShapeDtypeStruct(shape, BF16) for shape in outs]
    smem = pl.BlockSpec(memory_space=pltpu.SMEM)
    arrays = [tokens, *weights]
    return pl.pallas_call(
        functools.partial(first_kernel, shifts),
        out_shape=outs,
        grid=(1,),
        in_specs=[smem, smem] + [whole(a) for a in arrays],
        out_specs=[whole(o) for o in outs],
        compiler_params=params(60),
        cost_estimate=cost(100000000000),
        name="first_step",
    )(start, shift, *arrays)


def step_kernel(wide, sends, start, weight, on, back, *refs):
    others, outs = (refs[:-3], refs[-3:]) if len(refs) > 2 else ((), refs)
    height = on.shape[0]
    window = pl.ds(pl.multiple_of(start[0], LANES), weight.shape[0])
    piece = jnp.concatenate([on[:, window], back[:, window]], axis=0)
    value = jnp.dot(piece, weight[...], preferred_element_type=F32)
    for i, arrived in enumerate((on, back)):
        part = value[i * height : (i + 1) * height] + arrived[:, wide:].astype(F32)
        if sends[i]:
            outs[i][:, :wide] = arrived[:, :wide]
            outs[i][:, wide:] = part.astype(BF16)
        else:
            outs[i][...] = part.astype(BF16)
    if others:
        at = 0
        for r in (*others, on, back):
            outs[2][at : at + r.shape[0], :] = r[:, :wide]
            at += r.shape[0]


def step_on(start, weight, on, back, wide, sends, others):
    height, width = on.shape[0], weight.shape[1]
    vmem = pl.BlockSpec(memory_space=pltpu.VMEM)
    shapes = [(height, wide + width) if full else (height, width) for full in sends]
    if others:
        shapes.append((sum(o.shape[0] for o in others) + 2 * height, wide))
    return pl.pallas_call(
        functools.partial(step_kernel, wide, sends),
        out_shape=[jax.ShapeDtypeStruct(shape, BF16) for shape in shapes],
        in_specs=[pl.BlockSpec(memory_space=pltpu.SMEM)] + [vmem] * (3 + len(others)),
        out_specs=[vmem] * len(shapes),
        compiler_params=params(16),
        cost_estimate=cost(10000000000),
        name="step_on",
    )(start, weight, on, back, *others)


def open_kernel(start, weight, *refs):
    on, back, terms, outs = refs[:2], refs[2:4], refs[4], refs[5:]
    pair = outs[2]
    height, wide = on[0].shape
    window = pl.ds(pl.multiple_of(start[0], LANES), weight.shape[0])
    piece = jnp.concatenate([r[:, window] for r in (*on, *back)], axis=0)
    value = jnp.dot(piece, weight[...], preferred_element_type=F32)
    terms[...] = value[: 2 * height]
    for i, r in enumerate(back):
        outs[i][:, :wide] = r[...]
        outs[i][:, wide:] = value[(2 + i) * height : (3 + i) * height].astype(BF16)
    for i, r in enumerate((on[0], back[0], on[1], back[1])):
        pair[i * height : (i + 1) * height, :] = r[...]


def open_step(start, weight, on, back):
    height, wide = on[0].shape
    width = weight.shape[1]
    outs = [jax.ShapeDtypeStruct((2 * height, width), F32)]
    outs += [jax.ShapeDtypeStruct((height, wide + width), BF16)] * 2
    outs += [jax.ShapeDtypeStruct((4 * height, wide), BF16)]
    vmem = pl.BlockSpec(memory_space=pltpu.VMEM)
    return pl.pallas_call(
        open_kernel,
        out_shape=outs,
        in_specs=[pl.BlockSpec(memory_space=pltpu.SMEM)] + [vmem] * 5,
        out_specs=[vmem] * 4,
        compiler_params=params(16),
        cost_estimate=cost(100000000000),
        name="open_step",
    )(start, weight, *on, *back)


def onward_kernel(terms, sums, *refs):
    on, outs = refs[:2], refs[2:]
    height, wide = on[0].shape
    for i, r in enumerate(on):
        here = slice(i * height, (i + 1) * height)
        outs[i][:, :wide] = r[...]
        outs[i][:, wide:] = (terms[here, :] + sums[here, :].astype(F32)).astype(BF16)


def onward_step(terms, sums, on):
    height, wide = on[0].shape
    vmem = pl.BlockSpec(memory_space=pltpu.VMEM)
    out = jax.ShapeDtypeStruct((height, wide + sums.shape[1]), BF16)
    return pl.pallas_call(
        onward_kernel,
        out_shape=[out] * 2,
        in_specs=[vmem] * 4,
        out_specs=[vmem] * 2,
        compiler_params=params(16),
        cost_estimate=cost(10000000000),
        name="onward_step",
    )(terms, sums, *on)


def last_kernel(wide, start, weight, main, side, *refs):
    others, (units, *tokens) = (refs[:1], refs[1:]) if len(refs) == 3 else ((), refs)
    height = main.shape[0]
    window = pl.ds(pl.multiple_of(start[0], LANES), weight.shape[0])
    value = jnp.dot(main[:, window], weight[...], preferred_element_type=F32)
    value = value + main[:, wide:].astype(F32) + side[...].astype(F32)
    half = value.shape[1] // 2
    units[...] = (silu(value[:, :half]) * value[:, half:]).astype(BF16)
    if others:
        for i, r in enumerate((*others, main)):
            tokens[0][i * height : (i + 1) * height, :] = r[:, :wide]


def last_step(start, weight, main, side, wide, others=()):
    height = main.shape[0]
    vmem = pl.BlockSpec(memory_space=pltpu.VMEM)
    return pl.pallas_call(
        functools.partial(last_kernel, wide),
        out_shape=[jax.ShapeDtypeStruct((height, weight.shape[1] // 2), BF16)]
        + [jax.ShapeDtypeStruct((2 * height, wide), BF16)] * len(others),
        in_specs=[pl.BlockSpec(memory_space=pltpu.SMEM)] + [vmem] * (3 + len(others)),
        out_specs=[vmem] * (1 + len(others)),
        compiler_params=params(16),
        cost_estimate=cost(7000000000),
        name="last_step",
    )(start, weight, main, side, *others)


def merge_kernel(count, *refs):
    spreads, rows, owns = refs[:count], refs[count : 2 * count], refs[2 * count : 3 * count]
    other = refs[3 * count]
    for i in range(count):
        height, features = owns[i].shape
        which = spreads[i][...]
        for at, width in column_tiles(features):
            value = jnp.concatenate(
                [rows[i][e, :, at : at + width] for e in range(rows[i].shape[0])], axis=0
            )
            value = jnp.dot(which, value, preferred_element_type=F32)
            owns[i][:, at : at + width] = value[:height]
            other[i * height : (i + 1) * height, at : at + width] = value[height:].astype(BF16)


def merge_rows(spreads, rows):
    height, features = spreads[0].shape[0] // 2, rows[0].shape[2]
    count = len(rows)
    outs = [jax.ShapeDtypeStruct((height, features), F32)] * count
    outs.append(jax.ShapeDtypeStruct((count * height, features), BF16))
    arrays = [*spreads, *rows]
    return pl.pallas_call(
        functools.partial(merge_kernel, count),
        out_shape=outs,
        grid=(1,),
        in_specs=[whole(a) for a in arrays],
        out_specs=[whole(o) for o in outs],
        compiler_params=params(36),
        cost_estimate=cost(1000),
        name="merge_rows",
    )(*arrays)


def add_kernel(places, base, counts, joined, narrow, start, own, other, down, *refs):
    arrived, outs, total = refs[: sum(counts)], refs[sum(counts) : -1], refs[-1]
    features = own.shape[1]
    height = total.shape[0] // len(places)
    window = pl.ds(pl.multiple_of(start[0], LANES), down.shape[0])
    units = []
    for i, at in enumerate(places):
        mine = arrived[sum(counts[:i]) : sum(counts[: i + 1])]
        here = slice(i * height, (i + 1) * height)
        value = other[base + at : base + at + height, :].astype(F32)
        value = value + own[at : at + height, :]
        for a in mine:
            if a.shape[1] > features:
                value = value + a[:, :features].astype(F32)
        total[here, :] = value
        wide = mine[0].shape[1]
        units.append(mine[0][:, features:] if wide > features else mine[0][...])
    value = lax.dot_general(
        jnp.concatenate(units, axis=0),
        down[...],
        (((1,), (1,)), ((), ())),
        preferred_element_type=F32,
    )
    total[:, window] = total[:, window] + value
    if joined:
        outs[0][...] = total[...]
    else:
        for i, out in enumerate(outs):
            out[:, :features] = total[i * height : (i + 1) * height, :].astype(BF16)
            if not narrow:
                out[:, features:] = units[i]


def add_step(start, term, down, places, arrived, joined=False, narrow=False):
    own, other, base = term
    features = own.shape[1]
    counts = [len(a) for a in arrived]
    height = arrived[0][0].shape[0]
    count = len(places)
    vmem = pl.BlockSpec(memory_space=pltpu.VMEM)
    if joined:
        outs = [jax.ShapeDtypeStruct((count * height, features), F32)]
    else:
        shape = (height, features + (0 if narrow else down.shape[1]))
        outs = [jax.ShapeDtypeStruct(shape, BF16)] * count
    return pl.pallas_call(
        functools.partial(add_kernel, places, base, counts, joined, narrow),
        out_shape=outs,
        in_specs=[pl.BlockSpec(memory_space=pltpu.SMEM)] + [vmem] * (3 + sum(counts)),
        out_specs=[vmem] * len(outs),
        scratch_shapes=[pltpu.VMEM((count * height, features), F32)],
        compiler_params=params(16),
        cost_estimate=cost(100000000000),
        name="add_step",
    )(start, own, other, down, *[a for b in arrived for a in b])


def join_kernel(sums, first, second, out):
    height, features = first.shape[0], out.shape[1]
    for i, r in enumerate((first, second)):
        here = slice(i * height, (i + 1) * height)
        out[here, :] = (sums[here, :] + r[:, :features].astype(F32)).astype(BF16)


def join(sums, arrived):
    vmem = pl.BlockSpec(memory_space=pltpu.VMEM)
    return pl.pallas_call(
        join_kernel,
        out_shape=jax.ShapeDtypeStruct(sums.shape, BF16),
        in_specs=[vmem] * 3,
        out_specs=vmem,
        compiler_params=params(16),
        cost_estimate=cost(100000000000),
        name="join",
    )(sums, *arrived)


def window_width(count, size, total):
    need = max((i * size) % LANES + size for i in range(count))
    return min(total, -(-need // LANES) * LANES)


def on_device(
    tokens,
    route_ids,
    route_gates,
    expert_gate,
    expert_up,
    expert_down,
    shared_gate,
    shared_up,
    shared_down,
):
    n = lax.axis_size("expert")
    half = n // 2
    me = lax.axis_index("expert")
    row_count, features = tokens.shape
    top = route_ids.shape[1]
    experts = expert_gate.shape[0]
    slots = -(-4 * MOST // 16) * 16

    path = list(range(0, n, 2)) + list(range(n - 1, 0, -2))
    onward = [(path[i], path[(i + 1) % n]) for i in range(n)]
    backward = [(b, a) for a, b in onward]
    send_on = lambda a: lax.ppermute(a, "expert", onward)
    send_back = lambda a: lax.ppermute(a, "expert", backward)
    swap = lambda a: lax.ppermute(a, "tensor", [(0, 1), (1, 0)])

    first = (me * experts).reshape(1)

    size = shared_gate.shape[0]
    width = window_width(n, size, features)
    start = jnp.minimum(me * size // LANES * LANES, features - width)
    shift = (me * size - start).reshape(1)
    start = start.reshape(1)
    shifts = {i * size - min(i * size // LANES * LANES, features - width) for i in range(n)}
    weights = [f for w in (shared_gate, shared_up, shared_down.T) for f in (w, swap(w))]
    after = lambda x, y: lax.optimization_barrier((x, y))[0]
    split = row_count // 2
    *parts, tokens = note_tokens(tokens, route_ids.T, route_gates.T)
    wide = tokens.shape[1]
    ahead, behind = [send_on(p) for p in parts], [send_back(p) for p in parts]
    own = swap(tokens)
    first_start = after(start, own)
    both, down, sums = first_step(first_start, shift, sorted(shifts), tokens, weights, width)
    sums = send_on(sums)
    pick = lambda arrays, work=10000000000: pick_rows(first, arrays, experts, slots, top, work)
    pairs, picked = {}, {}
    terms, *sends, pair = open_step(after(start, down), both, ahead, behind)
    pairs[1] = [pair, swap(pair)]
    behind = [send_back(m) for m in sends]
    sends = onward_step(terms, sums, ahead)
    ahead = [send_on(m) for m in sends]
    done = sends[0]
    for k in range(2, half):
        others = []
        for stream in (0, 1):
            full = (k < half - 1 or stream == 0, k < half - 1 or stream == 1)
            on, back = ahead[stream], behind[stream]
            sends = step_on(after(start, done), both, on, back, wide, full, others)
            done = sends[0]
            ahead[stream], behind[stream] = send_on(sends[0]), send_back(sends[1])
            others = [on, back]
            if stream == 0:
                picked[k - 1] = pick([after(pairs[k - 1][0], done), pairs[k - 1][1]])
                done = picked[k - 1][1]
        pairs[k] = [sends[2], swap(sends[2])]
    main = [ahead[0], behind[1]]
    [upper] = last_step(after(start, done), both, main[0], behind[0], wide)
    k = half - 1
    picked[k] = pick([after(pairs[k][0], upper), pairs[k][1]], work=1000)
    done = picked[k][1]
    lower, end = last_step(after(start, done), both, main[1], ahead[1], wide, main[:1])
    units = upper, lower
    picked[0] = pick([tokens, end, own, swap(end)])

    lag = send_on(units[1]), send_back(units[0])
    routed = {}
    for at in range(0, half, 4):
        group = list(range(at, min(at + 4, half)))
        rows = [picked[j][0] for j in group]
        weights = expert_gate, expert_up, expert_down
        routed.update(zip(group, run_experts(first, rows, *weights, top)))

    def terms_of(chunks, done):
        spreads = [picked[c][1] for c in chunks]
        spreads[0] = after(spreads[0], done)
        *owns, other = merge_rows(spreads, [routed[c] for c in chunks])
        other = swap(other)
        return {c: (own, other, i * block) for i, (c, own) in enumerate(zip(chunks, owns))}

    block = 2 * row_count
    terms = terms_of([0], routed[0])
    terms.update(terms_of([half - 1], terms[0][0]))
    places, done = (row_count, row_count + split), terms[half - 1][0]
    lead = add_step(after(start, done), terms[0], down, places, [[units[0]], [units[1]]])
    done = lead[0]
    lead = send_on(lead[0]), send_back(lead[1])
    for k in range(half - 1, 0, -1):
        lag = add_step(after(start, done), terms[k], down, (3 * split, 0), [[lag[0]], [lag[1]]])
        done = lag[0]
        lag = send_on(lag[0]), send_back(lag[1])
        if k > 1 and k - 1 not in terms:
            terms.update(terms_of([k - 1, k - 2] if k > 2 else [k - 1], done))
            done = terms[k - 1][0]
        places, arrived = (split, 2 * split), [[lead[0]], [lead[1]]]
        lead = add_step(after(start, done), terms[k], down, places, arrived, narrow=k == 1)
        done = lead[0]
        lead = send_on(lead[0]), send_back(lead[1])
    arrived = [[lag[1]], [lag[0]]]
    [sums] = add_step(after(start, done), terms[0], down, (0, split), arrived, joined=True)
    return join(sums, lead)


def solution(mesh):
    in_specs = (
        P(("group", "expert", "tensor"), None),
        P(("group", "expert", "tensor"), None),
        P(("group", "expert", "tensor"), None),
        P("expert", None, "tensor"),
        P("expert", None, "tensor"),
        P("expert", "tensor", None),
        P("expert", "tensor"),
        P("expert", "tensor"),
        P("tensor", "expert"),
    )
    out_specs = P(("group", "expert", "tensor"), None)
    return jax.shard_map(
        on_device, mesh=mesh, in_specs=in_specs, out_specs=out_specs, check_vma=False
    )
```

```python
import functools

import jax
import jax.numpy as jnp
from jax import lax
from jax.experimental import pallas as pl
from jax.experimental.pallas import tpu as pltpu
from jax.sharding import PartitionSpec as P

MOST = 18
LANES = 128
MIB = 1 << 20
BF16 = jnp.bfloat16
F32 = jnp.float32


def cost(flops):
    return pl.CostEstimate(flops=flops, bytes_accessed=1000, transcendentals=0)


def params(mib):
    return pltpu.CompilerParams(vmem_limit_bytes=mib * MIB)


def column_tiles(total, width=512):
    return [(at, min(width, total - at)) for at in range(0, total, width)]


def silu(value):
    return value * (1.0 / (1.0 + jnp.exp(-value)))


def whole(array):
    return pl.BlockSpec(array.shape, lambda i: (0,) * array.ndim)


def pick_kernel(count, experts, top, first, *refs):
    tokens, out, spread = refs[:count], refs[count], refs[count + 1]
    features = out.shape[2]
    height, slots = spread.shape
    notes = jnp.concatenate([t[:, features - LANES :] for t in tokens], axis=0).astype(F32)
    lane = lax.broadcasted_iota(jnp.int32, notes.shape, 1)
    named = jnp.zeros(notes.shape, F32)
    for e in range(experts):
        same = (notes == (first[0] + e).astype(F32)) & (lane < top)
        hit = jnp.max(jnp.where(same, 1.0, 0.0), axis=1, keepdims=True)
        named = jnp.where(lane == e, hit, named)
    down = lax.broadcasted_iota(jnp.int32, (height, height), 0)
    across = lax.broadcasted_iota(jnp.int32, (height, height), 1)
    upto = jnp.where(across <= down, 1.0, 0.0).astype(BF16)
    rank = jnp.dot(upto, named.astype(BF16), preferred_element_type=F32).astype(jnp.int32) - 1
    slot = jnp.where(named > 0.0, rank + lane * (slots // experts), -1)
    turned = jnp.transpose(slot.astype(F32)).astype(jnp.int32)
    number = lax.broadcasted_iota(jnp.int32, (slots, height), 0)
    column = lax.broadcasted_iota(jnp.int32, (height, slots), 1)
    picks = number == turned[0:1, :]
    back = column == slot[:, 0:1]
    for e in range(1, experts):
        picks = picks | (number == turned[e : e + 1, :])
        back = back | (column == slot[:, e : e + 1])
    picks = jnp.where(picks, 1.0, 0.0).astype(BF16)
    spread[...] = jnp.where(back, 1.0, 0.0).astype(BF16)
    for at, width in column_tiles(features):
        piece = jnp.concatenate([t[:, at : at + width] for t in tokens], axis=0)
        rows = jnp.dot(picks, piece, preferred_element_type=F32).astype(BF16)
        out[:, :, at : at + width] = rows.reshape(experts, slots // experts, width)


def pick_rows(first, tokens, experts, slots, top, work):
    height = sum(t.shape[0] for t in tokens)
    features = tokens[0].shape[1]
    vmem = pl.BlockSpec(memory_space=pltpu.VMEM)
    return pl.pallas_call(
        functools.partial(pick_kernel, len(tokens), experts, top),
        out_shape=[
            jax.ShapeDtypeStruct((experts, slots, features), BF16),
            jax.ShapeDtypeStruct((height, experts * slots), BF16),
        ],
        in_specs=[pl.BlockSpec(memory_space=pltpu.SMEM)] + [vmem] * len(tokens),
        out_specs=[vmem, vmem],
        compiler_params=params(16),
        cost_estimate=cost(work),
        name="pick_rows",
    )(first, *tokens)


def expert_kernel(count, pieces, top, first, *refs):
    rows_in, weights = refs[:count], refs[count : count + 3]
    rows_out, refs = refs[count + 3 : 2 * count + 3], refs[2 * count + 3 :]
    rows, held, sems, piece_sems = refs[0], refs[1:4], refs[4], refs[5]
    slots, wide = rows_in[0].shape[1:]
    features = held[0].shape[1]
    here = pl.program_id(0)
    last = pl.num_programs(0) - 1
    depth = features // pieces

    def fetch(expert, which):
        slot = lax.rem(expert, 2)
        copy = pltpu.make_async_copy
        return copy(weights[which].at[expert], held[which].at[slot], sems.at[slot, which])

    def fetch_piece(at, which):
        part = pl.ds(at * depth, depth)
        copy = pltpu.make_async_copy
        return copy(weights[which].at[0, part], held[which].at[0, part], piece_sems.at[at, which])

    @pl.when(here == 0)
    def _():
        for at in range(pieces):
            for which in range(2):
                fetch_piece(at, which).start()
        fetch(0, 2).start()

    for i, r in enumerate(rows_in):
        rows[i * slots : (i + 1) * slots, :] = r[here]
    notes = rows[:, features:].astype(F32)
    lane = lax.broadcasted_iota(jnp.int32, notes.shape, 1)
    expert = (first[0] + here).astype(F32)
    chosen = jnp.where((notes == expert) & (lane < top), 1.0, 0.0)
    scale = jnp.zeros((notes.shape[0], 1), F32)
    for part in (1, 2, 3):
        moved = jnp.concatenate([notes[:, part * top :], notes[:, : part * top]], axis=1)
        scale = scale + jnp.sum(chosen * moved, axis=1, keepdims=True)

    def finish(gated, upward, down):
        hidden = (silu(gated) * upward * scale).astype(BF16)
        for at, width in column_tiles(features):
            done = jnp.dot(hidden, down[:, at : at + width], preferred_element_type=F32)
            done = done.astype(BF16)
            for i, r in enumerate(rows_out):
                r[here, :, at : at + width] = done[i * slots : (i + 1) * slots]

    @pl.when(here == 0)
    def _():
        gated = upward = None
        for at in range(pieces):
            for which in range(2):
                fetch_piece(at, which).wait()
            if at == 1:

                @pl.when(here < last)
                def _():
                    for which in range(3):
                        fetch(1, which).start()

            part = slice(at * depth, (at + 1) * depth)
            value = rows[:, part]
            g = jnp.dot(value, held[0][0, part], preferred_element_type=F32)
            u = jnp.dot(value, held[1][0, part], preferred_element_type=F32)
            gated, upward = (g, u) if at == 0 else (gated + g, upward + u)

        fetch(0, 2).wait()
        finish(gated, upward, held[2].at[0])

    @pl.when(here > 0)
    def _():
        @pl.when(here < last)
        def _():
            for which in range(3):
                fetch(here + 1, which).start()

        slot = lax.rem(here, 2)
        for which in range(2):
            fetch(here, which).wait()
        value = rows[:, :features]
        gated = jnp.dot(value, held[0][slot], preferred_element_type=F32)
        upward = jnp.dot(value, held[1][slot], preferred_element_type=F32)
        fetch(here, 2).wait()
        finish(gated, upward, held[2].at[slot])


def run_experts(first, rows, gate, up, down, top):
    experts, slots, wide = rows[0].shape
    features, hidden = gate.shape[1:]
    count = len(rows)
    height = count * slots
    pieces = 7
    vmem = pl.BlockSpec(memory_space=pltpu.VMEM)
    rows = [pltpu.with_memory_space_constraint(r, pltpu.VMEM) for r in rows]
    weights = [pltpu.with_memory_space_constraint(w, pltpu.HBM) for w in (gate, up, down)]
    return pl.pallas_call(
        functools.partial(expert_kernel, count, pieces, top),
        out_shape=[pltpu.VMEM((experts, slots, features), BF16)] * count,
        grid=(experts,),
        in_specs=[pl.BlockSpec(memory_space=pltpu.SMEM)]
        + [vmem] * count
        + [pl.BlockSpec(memory_space=pl.ANY)] * 3,
        out_specs=[vmem] * count,
        scratch_shapes=[pltpu.VMEM((height, wide), BF16)]
        + [pltpu.VMEM((2, *w.shape[1:]), BF16) for w in (gate, up, down)]
        + [pltpu.SemaphoreType.DMA((2, 3)), pltpu.SemaphoreType.DMA((pieces, 2))],
        compiler_params=params(28),
        cost_estimate=cost(100000000000),
        name="run_experts",
    )(first, *rows, *weights)


def note_kernel(tokens, ids, gates, *sends):
    rows, features = tokens.shape
    gate = gates[...]
    high = gate.astype(BF16).astype(F32)
    middle = (gate - high).astype(BF16).astype(F32)
    low = gate - high - middle
    notes = [ids[...].astype(F32), high, middle, low]
    notes.append(jnp.zeros((LANES - 4 * ids.shape[0], rows), F32))
    notes = jnp.transpose(jnp.concatenate(notes, axis=0)).astype(BF16)
    split = rows // 2
    for i, out in enumerate(sends):
        here = slice(i * split, (i + 1) * split) if i < 2 else slice(0, rows)
        out[:, :features] = tokens[here, :]
        out[:, features:] = notes[here]


def note_tokens(tokens, ids, gates):
    rows, wide = tokens.shape[0], tokens.shape[1] + LANES
    outs = [jax.ShapeDtypeStruct((r, wide), BF16) for r in (rows // 2, rows // 2, rows)]
    return pl.pallas_call(
        note_kernel,
        out_shape=outs,
        grid=(1,),
        in_specs=[whole(a) for a in (tokens, ids, gates)],
        out_specs=[whole(o) for o in outs],
        compiler_params=params(60),
        cost_estimate=cost(1000),
        name="note_tokens",
    )(tokens, ids, gates)


def first_kernel(shifts, shift, *refs):
    parts, (weight, down) = refs[:6], refs[6:]
    height, width = parts[0].shape
    gap = weight.shape[0] - height
    for s in shifts:

        @pl.when(shift[0] == s)
        def _():
            for part, out, at in zip(parts, [weight] * 4 + [down] * 2, (0, 1, 2, 3, 0, 1)):
                size = part.shape[1]
                here = slice(at * size, (at + 1) * size)
                if s:
                    out[:s, here] = jnp.zeros((s, size), BF16)
                out[s : s + height, here] = part[...]
                if s < gap:
                    out[s + height :, here] = jnp.zeros((gap - s, size), BF16)


def sums_kernel(start, tokens, weight, sums):
    window = pl.ds(pl.multiple_of(start[0], LANES), weight.shape[0])
    value = jnp.dot(tokens[:, window], weight[...], preferred_element_type=F32)
    sums[...] = value.astype(BF16)


def first_sums(start, tokens, weight):
    vmem = pl.BlockSpec(memory_space=pltpu.VMEM)
    return pl.pallas_call(
        sums_kernel,
        out_shape=jax.ShapeDtypeStruct((tokens.shape[0], weight.shape[1]), BF16),
        in_specs=[pl.BlockSpec(memory_space=pltpu.SMEM), vmem, vmem],
        out_specs=vmem,
        compiler_params=params(16),
        cost_estimate=cost(10000000000),
        name="first_sums",
    )(start, tokens, weight)


def first_step(shift, shifts, weights, width):
    inner = weights[0].shape[1]
    outs = [(width, 4 * inner), (width, 2 * inner)]
    outs = [jax.ShapeDtypeStruct(shape, BF16) for shape in outs]
    smem = pl.BlockSpec(memory_space=pltpu.SMEM)
    arrays = list(weights)
    return pl.pallas_call(
        functools.partial(first_kernel, shifts),
        out_shape=outs,
        grid=(1,),
        in_specs=[smem] + [whole(a) for a in arrays],
        out_specs=[whole(o) for o in outs],
        compiler_params=params(60),
        cost_estimate=cost(100000000000),
        name="first_step",
    )(shift, *arrays)


def step_kernel(wide, sends, start, weight, on, back, *refs):
    others, outs = (refs[:-3], refs[-3:]) if len(refs) > 2 else ((), refs)
    height = on.shape[0]
    window = pl.ds(pl.multiple_of(start[0], LANES), weight.shape[0])
    piece = jnp.concatenate([on[:, window], back[:, window]], axis=0)
    value = jnp.dot(piece, weight[...], preferred_element_type=F32)
    for i, arrived in enumerate((on, back)):
        part = value[i * height : (i + 1) * height] + arrived[:, wide:].astype(F32)
        if sends[i]:
            outs[i][:, :wide] = arrived[:, :wide]
            outs[i][:, wide:] = part.astype(BF16)
        else:
            outs[i][...] = part.astype(BF16)
    if others:
        at = 0
        for r in (*others, on, back):
            outs[2][at : at + r.shape[0], :] = r[:, :wide]
            at += r.shape[0]


def step_on(start, weight, on, back, wide, sends, others):
    height, width = on.shape[0], weight.shape[1]
    vmem = pl.BlockSpec(memory_space=pltpu.VMEM)
    shapes = [(height, wide + width) if full else (height, width) for full in sends]
    if others:
        shapes.append((sum(o.shape[0] for o in others) + 2 * height, wide))
    return pl.pallas_call(
        functools.partial(step_kernel, wide, sends),
        out_shape=[jax.ShapeDtypeStruct(shape, BF16) for shape in shapes],
        in_specs=[pl.BlockSpec(memory_space=pltpu.SMEM)] + [vmem] * (3 + len(others)),
        out_specs=[vmem] * len(shapes),
        compiler_params=params(16),
        cost_estimate=cost(10000000000),
        name="step_on",
    )(start, weight, on, back, *others)


def open_kernel(start, weight, *refs):
    on, back, terms, outs = refs[:2], refs[2:4], refs[4], refs[5:]
    pair = outs[2]
    height, wide = on[0].shape
    window = pl.ds(pl.multiple_of(start[0], LANES), weight.shape[0])
    piece = jnp.concatenate([r[:, window] for r in (*on, *back)], axis=0)
    value = jnp.dot(piece, weight[...], preferred_element_type=F32)
    terms[...] = value[: 2 * height]
    for i, r in enumerate(back):
        outs[i][:, :wide] = r[...]
        outs[i][:, wide:] = value[(2 + i) * height : (3 + i) * height].astype(BF16)
    for i, r in enumerate((on[0], back[0], on[1], back[1])):
        pair[i * height : (i + 1) * height, :] = r[...]


def open_step(start, weight, on, back):
    height, wide = on[0].shape
    width = weight.shape[1]
    outs = [jax.ShapeDtypeStruct((2 * height, width), F32)]
    outs += [jax.ShapeDtypeStruct((height, wide + width), BF16)] * 2
    outs += [jax.ShapeDtypeStruct((4 * height, wide), BF16)]
    vmem = pl.BlockSpec(memory_space=pltpu.VMEM)
    return pl.pallas_call(
        open_kernel,
        out_shape=outs,
        in_specs=[pl.BlockSpec(memory_space=pltpu.SMEM)] + [vmem] * 5,
        out_specs=[vmem] * 4,
        compiler_params=params(16),
        cost_estimate=cost(100000000000),
        name="open_step",
    )(start, weight, *on, *back)


def onward_kernel(terms, sums, *refs):
    on, outs = refs[:2], refs[2:]
    height, wide = on[0].shape
    for i, r in enumerate(on):
        here = slice(i * height, (i + 1) * height)
        outs[i][:, :wide] = r[...]
        outs[i][:, wide:] = (terms[here, :] + sums[here, :].astype(F32)).astype(BF16)


def onward_step(terms, sums, on):
    height, wide = on[0].shape
    vmem = pl.BlockSpec(memory_space=pltpu.VMEM)
    out = jax.ShapeDtypeStruct((height, wide + sums.shape[1]), BF16)
    return pl.pallas_call(
        onward_kernel,
        out_shape=[out] * 2,
        in_specs=[vmem] * 4,
        out_specs=[vmem] * 2,
        compiler_params=params(16),
        cost_estimate=cost(10000000000),
        name="onward_step",
    )(terms, sums, *on)


def last_kernel(wide, start, weight, main, side, *refs):
    others, (units, *tokens) = (refs[:1], refs[1:]) if len(refs) == 3 else ((), refs)
    height = main.shape[0]
    window = pl.ds(pl.multiple_of(start[0], LANES), weight.shape[0])
    value = jnp.dot(main[:, window], weight[...], preferred_element_type=F32)
    value = value + main[:, wide:].astype(F32) + side[...].astype(F32)
    half = value.shape[1] // 2
    units[...] = (silu(value[:, :half]) * value[:, half:]).astype(BF16)
    if others:
        for i, r in enumerate((*others, main)):
            tokens[0][i * height : (i + 1) * height, :] = r[:, :wide]


def last_step(start, weight, main, side, wide, others=()):
    height = main.shape[0]
    vmem = pl.BlockSpec(memory_space=pltpu.VMEM)
    return pl.pallas_call(
        functools.partial(last_kernel, wide),
        out_shape=[jax.ShapeDtypeStruct((height, weight.shape[1] // 2), BF16)]
        + [jax.ShapeDtypeStruct((2 * height, wide), BF16)] * len(others),
        in_specs=[pl.BlockSpec(memory_space=pltpu.SMEM)] + [vmem] * (3 + len(others)),
        out_specs=[vmem] * (1 + len(others)),
        compiler_params=params(16),
        cost_estimate=cost(10000000000),
        name="last_step",
    )(start, weight, main, side, *others)


def merge_kernel(count, *refs):
    spreads, rows, owns = refs[:count], refs[count : 2 * count], refs[2 * count : 3 * count]
    other = refs[3 * count]
    for i in range(count):
        height, features = owns[i].shape
        which = spreads[i][...]
        for at, width in column_tiles(features):
            value = jnp.concatenate(
                [rows[i][e, :, at : at + width] for e in range(rows[i].shape[0])], axis=0
            )
            value = jnp.dot(which, value, preferred_element_type=F32)
            owns[i][:, at : at + width] = value[:height]
            other[i * height : (i + 1) * height, at : at + width] = value[height:].astype(BF16)


def merge_rows(spreads, rows):
    height, features = spreads[0].shape[0] // 2, rows[0].shape[2]
    count = len(rows)
    outs = [jax.ShapeDtypeStruct((height, features), F32)] * count
    outs.append(jax.ShapeDtypeStruct((count * height, features), BF16))
    arrays = [*spreads, *rows]
    return pl.pallas_call(
        functools.partial(merge_kernel, count),
        out_shape=outs,
        grid=(1,),
        in_specs=[whole(a) for a in arrays],
        out_specs=[whole(o) for o in outs],
        compiler_params=params(36),
        cost_estimate=cost(1000),
        name="merge_rows",
    )(*arrays)


def add_kernel(places, base, counts, joined, narrow, start, own, other, down, *refs):
    arrived, outs, total = refs[: sum(counts)], refs[sum(counts) : -1], refs[-1]
    features = own.shape[1]
    height = total.shape[0] // len(places)
    window = pl.ds(pl.multiple_of(start[0], LANES), down.shape[0])
    units = []
    for i, at in enumerate(places):
        mine = arrived[sum(counts[:i]) : sum(counts[: i + 1])]
        here = slice(i * height, (i + 1) * height)
        value = other[base + at : base + at + height, :].astype(F32)
        value = value + own[at : at + height, :]
        for a in mine:
            if a.shape[1] > features:
                value = value + a[:, :features].astype(F32)
        total[here, :] = value
        wide = mine[0].shape[1]
        units.append(mine[0][:, features:] if wide > features else mine[0][...])
    value = lax.dot_general(
        jnp.concatenate(units, axis=0),
        down[...],
        (((1,), (1,)), ((), ())),
        preferred_element_type=F32,
    )
    total[:, window] = total[:, window] + value
    if joined:
        outs[0][...] = total[...]
    else:
        for i, out in enumerate(outs):
            out[:, :features] = total[i * height : (i + 1) * height, :].astype(BF16)
            if not narrow:
                out[:, features:] = units[i]


def add_step(start, term, down, places, arrived, joined=False, narrow=False):
    own, other, base = term
    features = own.shape[1]
    counts = [len(a) for a in arrived]
    height = arrived[0][0].shape[0]
    count = len(places)
    vmem = pl.BlockSpec(memory_space=pltpu.VMEM)
    if joined:
        outs = [jax.ShapeDtypeStruct((count * height, features), F32)]
    else:
        shape = (height, features + (0 if narrow else down.shape[1]))
        outs = [jax.ShapeDtypeStruct(shape, BF16)] * count
    return pl.pallas_call(
        functools.partial(add_kernel, places, base, counts, joined, narrow),
        out_shape=outs,
        in_specs=[pl.BlockSpec(memory_space=pltpu.SMEM)] + [vmem] * (3 + sum(counts)),
        out_specs=[vmem] * len(outs),
        scratch_shapes=[pltpu.VMEM((count * height, features), F32)],
        compiler_params=params(16),
        cost_estimate=cost(100000000000),
        name="add_step",
    )(start, own, other, down, *[a for b in arrived for a in b])


def join_kernel(sums, first, second, out):
    height, features = first.shape[0], out.shape[1]
    for i, r in enumerate((first, second)):
        here = slice(i * height, (i + 1) * height)
        out[here, :] = (sums[here, :] + r[:, :features].astype(F32)).astype(BF16)


def join(sums, arrived):
    vmem = pl.BlockSpec(memory_space=pltpu.VMEM)
    return pl.pallas_call(
        join_kernel,
        out_shape=jax.ShapeDtypeStruct(sums.shape, BF16),
        in_specs=[vmem] * 3,
        out_specs=vmem,
        compiler_params=params(16),
        cost_estimate=cost(100000000000),
        name="join",
    )(sums, *arrived)


def window_width(count, size, total):
    need = max((i * size) % LANES + size for i in range(count))
    return min(total, -(-need // LANES) * LANES)


def on_device(
    tokens,
    route_ids,
    route_gates,
    expert_gate,
    expert_up,
    expert_down,
    shared_gate,
    shared_up,
    shared_down,
):
    n = lax.axis_size("expert")
    half = n // 2
    me = lax.axis_index("expert")
    row_count, features = tokens.shape
    top = route_ids.shape[1]
    experts = expert_gate.shape[0]
    slots = -(-4 * MOST // 16) * 16

    path = list(range(0, n, 2)) + list(range(n - 1, 0, -2))
    onward = [(path[i], path[(i + 1) % n]) for i in range(n)]
    backward = [(b, a) for a, b in onward]
    send_on = lambda a: lax.ppermute(a, "expert", onward)
    send_back = lambda a: lax.ppermute(a, "expert", backward)
    swap = lambda a: lax.ppermute(a, "tensor", [(0, 1), (1, 0)])

    first = (me * experts).reshape(1)

    size = shared_gate.shape[0]
    width = window_width(n, size, features)
    start = jnp.minimum(me * size // LANES * LANES, features - width)
    shift = (me * size - start).reshape(1)
    start = start.reshape(1)
    shifts = {i * size - min(i * size // LANES * LANES, features - width) for i in range(n)}
    weights = [f for w in (shared_gate, shared_up, shared_down.T) for f in (w, swap(w))]
    after = lambda x, y: lax.optimization_barrier((x, y))[0]
    split = row_count // 2
    *parts, tokens = note_tokens(tokens, route_ids.T, route_gates.T)
    wide = tokens.shape[1]
    ahead, behind = [send_on(p) for p in parts], [send_back(p) for p in parts]
    own = swap(tokens)
    both, down = first_step(after(shift, own), sorted(shifts), weights, width)
    sums = first_sums(start, tokens, both)
    done, sums = sums, send_on(sums)
    pick = lambda arrays, work=10000000000: pick_rows(first, arrays, experts, slots, top, work)
    pairs, picked = {}, {}
    terms, *sends, pair = open_step(after(start, done), both, ahead, behind)
    pairs[1] = [pair, swap(pair)]
    behind = [send_back(m) for m in sends]
    sends = onward_step(terms, sums, ahead)
    ahead = [send_on(m) for m in sends]
    done = sends[0]
    for k in range(2, half):
        others = []
        for stream in (0, 1):
            full = (k < half - 1 or stream == 0, k < half - 1 or stream == 1)
            on, back = ahead[stream], behind[stream]
            sends = step_on(after(start, done), both, on, back, wide, full, others)
            done = sends[0]
            ahead[stream], behind[stream] = send_on(sends[0]), send_back(sends[1])
            others = [on, back]
            if stream == 0:
                picked[k - 1] = pick([after(pairs[k - 1][0], done), pairs[k - 1][1]])
                done = picked[k - 1][1]
        pairs[k] = [sends[2], swap(sends[2])]
    main = [ahead[0], behind[1]]
    [upper] = last_step(after(start, done), both, main[0], behind[0], wide)
    k = half - 1
    picked[k] = pick([after(pairs[k][0], upper), pairs[k][1]], work=1000)
    done = picked[k][1]
    lower, end = last_step(after(start, done), both, main[1], ahead[1], wide, main[:1])
    units = upper, lower
    picked[0] = pick([tokens, end, own, swap(end)])

    lag = send_on(units[1]), send_back(units[0])
    routed = {}
    for at in range(0, half, 4):
        group = list(range(at, min(at + 4, half)))
        rows = [picked[j][0] for j in group]
        weights = expert_gate, expert_up, expert_down
        routed.update(zip(group, run_experts(first, rows, *weights, top)))

    def terms_of(chunks, done):
        spreads = [picked[c][1] for c in chunks]
        spreads[0] = after(spreads[0], done)
        *owns, other = merge_rows(spreads, [routed[c] for c in chunks])
        other = swap(other)
        return {c: (own, other, i * block) for i, (c, own) in enumerate(zip(chunks, owns))}

    block = 2 * row_count
    terms = terms_of([0], routed[0])
    terms.update(terms_of([half - 1], terms[0][0]))
    places, done = (row_count, row_count + split), terms[half - 1][0]
    lead = add_step(after(start, done), terms[0], down, places, [[units[0]], [units[1]]])
    done = lead[0]
    lead = send_on(lead[0]), send_back(lead[1])
    for k in range(half - 1, 0, -1):
        lag = add_step(after(start, done), terms[k], down, (3 * split, 0), [[lag[0]], [lag[1]]])
        done = lag[0]
        lag = send_on(lag[0]), send_back(lag[1])
        if k > 1 and k - 1 not in terms:
            terms.update(terms_of([k - 1, k - 2] if k > 2 else [k - 1], done))
            done = terms[k - 1][0]
        places, arrived = (split, 2 * split), [[lead[0]], [lead[1]]]
        lead = add_step(after(start, done), terms[k], down, places, arrived, narrow=k == 1)
        done = lead[0]
        lead = send_on(lead[0]), send_back(lead[1])
    arrived = [[lag[1]], [lag[0]]]
    [sums] = add_step(after(start, done), terms[0], down, (0, split), arrived, joined=True)
    return join(sums, lead)


def solution(mesh):
    in_specs = (
        P(("group", "expert", "tensor"), None),
        P(("group", "expert", "tensor"), None),
        P(("group", "expert", "tensor"), None),
        P("expert", None, "tensor"),
        P("expert", None, "tensor"),
        P("expert", "tensor", None),
        P("expert", "tensor"),
        P("expert", "tensor"),
        P("tensor", "expert"),
    )
    out_specs = P(("group", "expert", "tensor"), None)
    return jax.shard_map(
        on_device, mesh=mesh, in_specs=in_specs, out_specs=out_specs, check_vma=False
    )
```
